256 devices in a mesh: pipe: 16 (over z, x_lo), tensor: 8 (over y, core), dp: 2 (over x_hi).
Axes of the slice: x: 4 (x_hi: 2, x_lo: 2; x = x_hi * 2 + x_lo), y: 4, z: 8, core: 2. Of those that a mesh axis runs over, the one named last changes fastest.
Arguments:
- query_new: bfloat16 [32, 512, 6144], P(('dp', 'pipe'), 'tensor'), parts along dimension 0, may hold values from -19 to 19
- key_new: bfloat16 [32, 512, 6144], P(('dp', 'pipe'), 'tensor'), parts along dimension 0, may hold values from -19 to 19
- value_new: bfloat16 [32, 512, 6144], P(('dp', 'pipe'), 'tensor'), parts along dimension 0, may hold values from -6 to 6
- stash_held: bfloat16 [32, 2, 3, 512, 6144], P(('dp', 'pipe'), None, None, None, 'tensor'), parts along dimension 0, may hold values from -19 to 19
- fetch_slot: int32 [32], P('dp'), parts along dimension 0, may hold values from 0 to 1
- cotangent: bfloat16 [32, 512, 6144], P(('dp', 'pipe'), 'tensor'), parts along dimension 0, may hold values from -6 to 6
Outputs:
- received: bfloat16 [32, 512, 6144], P(('dp', 'pipe'), 'tensor'), parts along dimension 0
- gradients: bfloat16 [32, 3, 512, 6144], P(('dp', 'pipe'), None, 'tensor'), parts along dimension 0
- evicted: bfloat16 [32, 3, 512, 6144], P(('dp', 'pipe'), None, None, 'tensor'), parts along dimension 0
The draws below stay inside these ranges and needn't reach their ends.
There are 2 independent parts, one for each index of `dp`. The reference program is written for one: setup_inputs(seed, part) draws one part's arguments, and reference() takes and returns one part's arrays. A program takes and returns all parts, laid end to end along the dimension named above; each array names one. Nothing has to cross between parts.
All inputs are finite; a program needn't handle non-finite values.
Results may differ from the reference program's by a relative error of at most 0.0063.
Values may be sent and summed in bfloat16 or wider, within the bound.
No kernel may reach another device: no remote copies, remote signals or barrier semaphores. Data moves between devices by JAX's collectives and lax.ppermute only.
A program may use at most 128 MiB of HBM per device.

```python
import jax
import jax.numpy as jnp
from jax import lax

HD = 128
SEQ = 512
SLOTS = 2
SECTIONS = 16
FEAT = 6144


def drawn_pair(key, lead, lift):
    shape = lead + (SEQ, FEAT)
    split_keys = jax.random.split(key, 2)
    queries = jnp.clip(jax.random.normal(split_keys[0], shape, jnp.float32), -6.0, 6.0)
    key_rows = jnp.clip(jax.random.normal(split_keys[1], shape, jnp.float32), -6.0, 6.0)
    places = jnp.arange(SEQ)[:, None]
    query_mark = (places % 32 == 31).astype(jnp.float32) * lift
    near_mark = (places % 32 == 26).astype(jnp.float32) * lift
    queries = queries * (1.0 - query_mark)
    key_rows = key_rows * (1.0 - near_mark)
    return (queries, key_rows)


def draw_query_new(key, part):
    lift = 0.0
    queries, key_rows = drawn_pair(key, (SECTIONS,), lift)
    return queries.astype(jnp.bfloat16)


def draw_key_new(key, part):
    lift = 0.0
    queries, key_rows = drawn_pair(key, (SECTIONS,), lift)
    return key_rows.astype(jnp.bfloat16)


def draw_stash_held(key, part):
    key = jax.random.fold_in(key, 7)
    lift = 0.0
    queries, key_rows = drawn_pair(jax.random.fold_in(key, 3), (SECTIONS, SLOTS), lift)
    values = jnp.clip(jax.random.normal(jax.random.fold_in(key, 11), (SECTIONS, SLOTS, SEQ, FEAT), jnp.float32), -6.0, 6.0)
    return jnp.stack([queries, key_rows, values], axis=2).astype(jnp.bfloat16)


def place_ends(result, rng, least, largest):
    extent = result.shape
    index_at = [jax.random.randint(jax.random.fold_in(rng, axis), (), 0, extent[axis]) for axis in range(len(extent))]
    result = result.at[tuple(index_at)].set(least)
    longest = extent.index(max(extent))
    index_at[longest] = (index_at[longest] + 1) % extent[longest]
    return result.at[tuple(index_at)].set(largest)


def block_scale(own_key, dims, cuts, smallest, high):
    def one(position, parts):
        steps = jax.random.uniform(jax.random.fold_in(jax.random.fold_in(own_key, 6), position), (parts,), jnp.float32, smallest / len(cuts), high / len(cuts))
        return jnp.repeat(jnp.exp(steps), dims[position] // parts).reshape((-1,) + (1,) * (len(dims) - position - 1))

    level = one(*cuts[0])
    for cut in cuts[1:]:
        level = level * one(*cut)
    return level


def scatter_about(key, shape, width, reach, shards=(), held_as=jnp.bfloat16):
    loudness = block_scale(key, shape, shards, -0.22, 0.18) if shards else 1.0
    entries = jax.random.normal(key, shape, jnp.float32) * width * loudness
    return jnp.minimum(jnp.maximum(entries, -reach), reach).astype(held_as)


def setup_inputs(seed: int = 0, part: int = 0) -> dict:
    arg_keys = jax.random.split(jax.random.key(seed), 7)
    part_keys = jax.random.split(jax.random.fold_in(arg_keys[6], part), 7)
    query_new = draw_query_new(jax.random.fold_in(jax.random.fold_in(arg_keys[6], part), 71), part)
    key_new = draw_key_new(jax.random.fold_in(jax.random.fold_in(arg_keys[6], part), 71), part)
    value_new = scatter_about(part_keys[2], (SECTIONS, SEQ, FEAT), 1.0, 6.0, ((0, 16), (1, 8)))
    stash_held = draw_stash_held(jax.random.fold_in(jax.random.fold_in(arg_keys[6], part), 71), part)
    fetch_slot = place_ends(jax.random.randint(part_keys[4], (SECTIONS,), 0, SLOTS), jax.random.fold_in(part_keys[4], 1), 0, SLOTS - 1).astype(jnp.int32)
    cotangent = scatter_about(part_keys[5], (SECTIONS, SEQ, FEAT), 1.0, 6.0, ((0, 16), (1, 8)))
    return {"query_new": query_new, "key_new": key_new, "value_new": value_new, "stash_held": stash_held, "fetch_slot": fetch_slot, "cotangent": cotangent}


def probabilities(queries, key_rows):
    length = queries.shape[0]
    query_heads = queries.reshape(length, -1, HD).astype(jnp.float32)
    key_heads = key_rows.reshape(length, -1, HD).astype(jnp.float32)
    scores = jnp.einsum("qhd,khd->hqk", query_heads, key_heads) * (HD ** -0.5)
    places = jnp.arange(length)
    scores = jnp.where(places[None, :] <= places[:, None], scores, -1e30)
    maximum = jnp.max(scores, axis=-1, keepdims=True)
    shifted = jnp.exp(scores - maximum)
    return shifted / jnp.sum(shifted, axis=-1, keepdims=True)


def forward_core(queries, key_rows, values):
    length = queries.shape[0]
    probs = probabilities(queries, key_rows)
    rounded = lax.optimization_barrier(probs.astype(jnp.bfloat16)).astype(jnp.float32)
    value_heads = values.reshape(length, -1, HD).astype(jnp.float32)
    output = jnp.einsum("hqk,khd->qhd", rounded, value_heads)
    return output.reshape(length, -1).astype(jnp.bfloat16)


def backward_core(queries, key_rows, values, upstream):
    length = queries.shape[0]
    probs = probabilities(queries, key_rows)
    rounded = lax.optimization_barrier(probs.astype(jnp.bfloat16)).astype(jnp.float32)
    query_heads = queries.reshape(length, -1, HD).astype(jnp.float32)
    key_heads = key_rows.reshape(length, -1, HD).astype(jnp.float32)
    value_heads = values.reshape(length, -1, HD).astype(jnp.float32)
    grad_heads = upstream.reshape(length, -1, HD).astype(jnp.float32)
    grad_values = jnp.einsum("hqk,qhd->khd", rounded, grad_heads)
    grad_probs = jnp.einsum("qhd,khd->hqk", grad_heads, value_heads)
    centre = jnp.sum(probs * grad_probs, axis=-1, keepdims=True)
    grad_scores = (probs * (grad_probs - centre) * (HD ** -0.5)).astype(jnp.bfloat16)
    grad_scores = lax.optimization_barrier(grad_scores).astype(jnp.float32)
    grad_queries = jnp.einsum("hqk,khd->qhd", grad_scores, key_heads)
    grad_keys = jnp.einsum("hqk,qhd->khd", grad_scores, query_heads)
    stacked = [grad_queries, grad_keys, grad_values]
    return jnp.stack([piece.reshape(length, -1).astype(jnp.bfloat16) for piece in stacked], axis=0)


def forward_group(group):
    return forward_core(group[0], group[1], group[2])


def backward_group(group):
    return backward_core(group[0][0], group[0][1], group[0][2], group[1])


def reference(query_new, key_new, value_new, stash_held, fetch_slot, cotangent):
    outputs = lax.map(forward_group, (query_new, key_new, value_new))
    received = jnp.concatenate([jnp.zeros_like(outputs[:1]), outputs[:-1]], axis=0)
    evicted = jnp.stack([query_new, key_new, value_new], axis=1)[::-1]
    partners = (SECTIONS - 1 - jnp.arange(SECTIONS)).astype(jnp.int32)
    fetched = stash_held[partners, fetch_slot.astype(jnp.int32)]
    upstream = jnp.roll(cotangent, -1, axis=0)
    gradients = lax.map(backward_group, (fetched, upstream))
    return received, gradients, evicted
```

```python
import jax
import jax.numpy as jnp
from jax import lax
from jax.experimental import pallas as pl
from jax.experimental.pallas import tpu as pltpu
from jax.sharding import PartitionSpec as P

HD = 128
SCALE = HD ** (-0.5)
ROWS = 256


def _nt(a, b):
    return lax.dot_general(a, b, (((1,), (1,)), ((), ())), preferred_element_type=jnp.float32)


def _nn(a, b):
    return lax.dot_general(a, b, (((1,), (0,)), ((), ())), preferred_element_type=jnp.float32)


def _tn(a, b):
    return lax.dot_general(a, b, (((0,), (0,)), ((), ())), preferred_element_type=jnp.float32)


def _probs(a, b, first):
    scores = _nt(a, b) * SCALE
    row = lax.broadcasted_iota(jnp.int32, scores.shape, 0) + first
    col = lax.broadcasted_iota(jnp.int32, scores.shape, 1)
    scores = jnp.where(col <= row, scores, -1e30)
    shifted = jnp.exp(scores - jnp.max(scores, axis=-1, keepdims=True))
    return shifted / jnp.sum(shifted, axis=-1, keepdims=True)


def _forward_kernel(x_ref, u_ref, o_ref, b_ref):
    chunks, parts, _, rows, _ = x_ref.shape
    part_rows = chunks * rows
    length = chunks * parts * rows
    for i in range(3):
        for j in range(chunks):
            for p in range(parts):
                b_ref[i, pl.ds(p * part_rows + j * rows, rows)] = x_ref[j, p, i]
    q, k, v = (b_ref[i] for i in range(3))
    feat = u_ref.shape[-1] // parts
    for p in range(parts):
        o_ref[p, 1] = u_ref[0, :, pl.ds(pl.multiple_of(p * feat + pl.program_id(0) * HD, HD), HD)]
    for first in range(0, length, ROWS):
        last = first + ROWS
        weights = _probs(q[first:last], k[:last], first).astype(jnp.bfloat16)
        out = _nn(weights, v[:last]).astype(jnp.bfloat16)
        o_ref[first // part_rows : last // part_rows, 0] = out.reshape(ROWS // part_rows, part_rows, HD)


def _backward_kernel(f_ref, g_ref, o_ref, dk_ref, dv_ref):
    parts, rows, _ = g_ref.shape
    length = parts * rows
    a, b, c = (f_ref[i] for i in range(3))
    g = g_ref[...].reshape(length, HD)

    def store(kind, first, x):
        x = x.astype(jnp.bfloat16).reshape(x.shape[0] // rows, rows, HD)
        o_ref[first // rows : first // rows + x.shape[0], kind] = x

    for first in reversed(range(0, length, ROWS)):
        last = first + ROWS
        probs = _probs(a[first:last], b[:last], first)
        grad_probs = _nt(g[first:last], c[:last])
        centre = jnp.sum(probs * grad_probs, axis=-1, keepdims=True)
        grad_scores = (probs * (grad_probs - centre) * SCALE).astype(jnp.bfloat16)
        store(0, first, _nn(grad_scores, b[:last]))
        dk = _tn(grad_scores, a[first:last])
        dv = _tn(probs.astype(jnp.bfloat16), g[first:last])
        if last == length:
            dk_ref[...] = dk
            dv_ref[...] = dv
        else:
            dk_ref[:last] += dk
            dv_ref[:last] += dv
    store(1, 0, dk_ref[...])
    store(2, 0, dv_ref[...])


HBM = pl.BlockSpec(memory_space=pltpu.HBM)
SMALL = pl.CostEstimate(flops=1, bytes_accessed=1, transcendentals=0)


def _move(kernel, out_shape, inputs, n, name, in_specs=None):
    return pl.pallas_call(
        kernel,
        in_specs=in_specs or [HBM] * len(inputs),
        out_specs=HBM,
        out_shape=jax.ShapeDtypeStruct(out_shape, jnp.bfloat16),
        scratch_shapes=[
            pltpu.VMEM(out_shape, jnp.bfloat16),
            pltpu.SemaphoreType.DMA((n,)),
            pltpu.SemaphoreType.DMA((n,)),
        ],
        compiler_params=pltpu.CompilerParams(vmem_limit_bytes=8 * 2**20),
        cost_estimate=SMALL,
        name=name,
    )(*inputs)


def _through(pairs, buf_ref, out_ref, in_sems, out_sems):
    into = [
        pltpu.make_async_copy(src, buf_ref.at[place], in_sems.at[i]) for i, (src, place) in enumerate(pairs)
    ]
    out = [
        pltpu.make_async_copy(buf_ref.at[place], out_ref.at[place], out_sems.at[i])
        for i, (_, place) in enumerate(pairs)
    ]
    for copy in into:
        copy.start()
    for first, second in zip(into, out):
        first.wait()
        second.start()
    for copy in out:
        copy.wait()


def held_block(fetch_slot, stash_held):
    _, _, n, length, feat = stash_held.shape

    def kernel(slot_ref, stash_ref, out_ref, buf_ref, in_sems, out_sems):
        slot = slot_ref[lax.axis_size("pipe") - 1 - lax.axis_index("pipe")]
        _through([(stash_ref.at[0, slot, i], i) for i in range(n)], buf_ref, out_ref, in_sems, out_sems)

    specs = [pl.BlockSpec(memory_space=pltpu.SMEM), HBM]
    return _move(kernel, (n, length, feat), (fetch_slot, stash_held), n, "held_block", specs)


def pack_tokens(arrays, parts, after=()):
    n = len(arrays)
    _, rows, feat = arrays[0].shape
    own, some = feat // parts, rows // 2

    def kernel(*refs):
        out_ref, buf_ref, in_sems, out_sems = refs[-4:]
        pairs = [
            (refs[i].at[0, pl.ds(j * some, some), pl.ds(p * own, own)], (j, p, i))
            for j in range(2)
            for p in range(parts)
            for i in range(n)
        ]
        _through(pairs, buf_ref, out_ref, in_sems, out_sems)

    return _move(kernel, (2, parts, n, some, own), (*arrays, *after), 2 * parts * n, "pack_tokens")


def unpack_tokens(x):
    parts, n, rows, own = x.shape

    def kernel(x_ref, out_ref, buf_ref, in_sems, out_sems):
        pairs = [(x_ref.at[p, i], (i, slice(None), pl.ds(p * own, own))) for p in range(parts) for i in range(n)]
        _through(pairs, buf_ref, out_ref, in_sems, out_sems)

    return _move(kernel, (n, rows, parts * own), (x,), parts * n, "unpack_tokens")


def forward_core(x, rows_up):
    chunks, parts, _, rows, feat = x.shape
    part_rows = chunks * rows
    return pl.pallas_call(
        _forward_kernel,
        grid=(feat // HD,),
        in_specs=[
            pl.BlockSpec((chunks, parts, 3, rows, HD), lambda h: (0, 0, 0, 0, h)),
            pl.BlockSpec(rows_up.shape, lambda h: (0, 0, 0)),
        ],
        out_specs=[
            pl.BlockSpec((parts, 2, part_rows, HD), lambda h: (0, 0, 0, h)),
            pl.BlockSpec((3, parts * part_rows, HD), lambda h: (0, 0, h)),
        ],
        out_shape=[
            jax.ShapeDtypeStruct((parts, 2, part_rows, feat), jnp.bfloat16),
            jax.ShapeDtypeStruct((3, parts * part_rows, feat), jnp.bfloat16),
        ],
        compiler_params=pltpu.CompilerParams(vmem_limit_bytes=24 * 2**20),
        cost_estimate=SMALL,
        name="forward_core",
    )(x, rows_up)


def backward_core(fetched, upstream, after):
    parts, rows, feat = upstream.shape
    length = parts * rows

    def kernel(f_ref, g_ref, _, *refs):
        _backward_kernel(f_ref, g_ref, *refs)

    return pl.pallas_call(
        kernel,
        grid=(feat // HD,),
        in_specs=[
            pl.BlockSpec((3, length, HD), lambda h: (0, 0, h)),
            pl.BlockSpec((parts, rows, HD), lambda h: (0, 0, h)),
            pl.BlockSpec(memory_space=pl.ANY),
        ],
        out_specs=pl.BlockSpec((parts, 3, rows, HD), lambda h: (0, 0, 0, h)),
        out_shape=jax.ShapeDtypeStruct((parts, 3, rows, feat), jnp.bfloat16),
        scratch_shapes=[pltpu.VMEM((length, HD), jnp.float32)] * 2,
        compiler_params=pltpu.CompilerParams(vmem_limit_bytes=24 * 2**20),
        cost_estimate=SMALL,
        name="backward_core",
    )(fetched, upstream, after)


def exchange(x):
    return lax.all_to_all(x, "tensor", split_axis=0, concat_axis=0, tiled=True)


def on_device(query_new, key_new, value_new, stash_held, fetch_slot, cotangent):
    sections = lax.axis_size("pipe")
    section = lax.axis_index("pipe")
    parts = lax.axis_size("tensor")
    mirror = [(s, sections - 1 - s) for s in range(sections)]

    upstream = lax.ppermute(cotangent, "pipe", [(s, (s - 1) % sections) for s in range(sections)])
    held = held_block(fetch_slot, stash_held)
    fetched = lax.ppermute(held, "pipe", mirror)

    packed = pack_tokens((query_new, key_new, value_new), parts, after=(held,))
    output, block = forward_core(lax.map(exchange, packed), upstream)
    both = exchange(output)
    output = lax.ppermute(both[:, 0], "pipe", [(s, s + 1) for s in range(sections - 1)])

    half = sections // 2
    steps = [(0, 2), (1, 3), (half - 2, half - 4), (half - 1, half - 3)]
    steps = steps + [(s + half, t + half) for s, t in steps]
    token = lax.ppermute(fetched[0, :16, :128], "pipe", steps)
    block, token, fetched = lax.optimization_barrier((block, token, fetched))
    evicted = lax.ppermute(block[None], "pipe", mirror)

    grads = backward_core(fetched, both[:, 1], token)
    grads, output = lax.optimization_barrier((grads, output))
    return unpack_tokens(output[:, None]), unpack_tokens(exchange(grads))[None], evicted


def solution(mesh):
    in_specs = (
        P(("dp", "pipe"), "tensor", None),
        P(("dp", "pipe"), "tensor", None),
        P(("dp", "pipe"), "tensor", None),
        P(("dp", "pipe"), None, None, None, "tensor"),
        P("dp"),
        P(("dp", "pipe"), "tensor", None),
    )
    out_specs = (
        P(("dp", "pipe"), "tensor", None),
        P(("dp", "pipe"), None, "tensor", None),
        P(("dp", "pipe"), None, None, "tensor"),
    )
    return jax.shard_map(
        on_device, mesh=mesh, in_specs=in_specs, out_specs=out_specs, check_vma=False
    )
```

```python
import jax
import jax.numpy as jnp
from jax import lax
from jax.experimental import pallas as pl
from jax.experimental.pallas import tpu as pltpu
from jax.sharding import PartitionSpec as P

HD = 128
SCALE = HD ** (-0.5)
ROWS = 256


def _nt(a, b):
    return lax.dot_general(a, b, (((1,), (1,)), ((), ())), preferred_element_type=jnp.float32)


def _nn(a, b):
    return lax.dot_general(a, b, (((1,), (0,)), ((), ())), preferred_element_type=jnp.float32)


def _tn(a, b):
    return lax.dot_general(a, b, (((0,), (0,)), ((), ())), preferred_element_type=jnp.float32)


def _probs(a, b, first):
    scores = _nt(a, b) * SCALE
    row = lax.broadcasted_iota(jnp.int32, scores.shape, 0) + first
    col = lax.broadcasted_iota(jnp.int32, scores.shape, 1)
    scores = jnp.where(col <= row, scores, -1e30)
    shifted = jnp.exp(scores - jnp.max(scores, axis=-1, keepdims=True))
    return shifted / jnp.sum(shifted, axis=-1, keepdims=True)


def _forward_kernel(x_ref, u_ref, o_ref, b_ref, c_ref):
    chunks, parts, _, rows, _ = x_ref.shape
    part_rows = chunks * rows
    length = chunks * parts * rows
    whole = []
    for i in range(3):
        blocks = [x_ref[j, p, i] for p in range(parts) for j in range(chunks)]
        whole.append(jnp.concatenate(blocks, axis=0))
    q, k, v = whole
    main = b_ref.shape[0] - 2 * length
    b_ref[:length] = q
    b_ref[length : 2 * length] = k
    b_ref[2 * length :] = v[:main]
    c_ref[...] = v[main:]
    feat = u_ref.shape[-1] // parts
    for p in range(parts):
        o_ref[p, 1] = u_ref[0, :, pl.ds(pl.multiple_of(p * feat + pl.program_id(0) * HD, HD), HD)]
    for first in range(0, length, ROWS):
        last = first + ROWS
        weights = _probs(q[first:last], k[:last], first).astype(jnp.bfloat16)
        out = _nn(weights, v[:last]).astype(jnp.bfloat16)
        o_ref[first // part_rows : last // part_rows, 0] = out.reshape(ROWS // part_rows, part_rows, HD)


def _backward_kernel(f_ref, g_ref, o_ref, dk_ref, dv_ref):
    parts, rows, _ = g_ref.shape
    length = parts * rows
    a, b, c = (f_ref[i] for i in range(3))
    g = g_ref[...].reshape(length, HD)

    def store(kind, first, x):
        x = x.astype(jnp.bfloat16).reshape(x.shape[0] // rows, rows, HD)
        o_ref[first // rows : first // rows + x.shape[0], kind] = x

    for first in reversed(range(0, length, ROWS)):
        last = first + ROWS
        probs = _probs(a[first:last], b[:last], first)
        grad_probs = _nt(g[first:last], c[:last])
        centre = jnp.sum(probs * grad_probs, axis=-1, keepdims=True)
        grad_scores = (probs * (grad_probs - centre) * SCALE).astype(jnp.bfloat16)
        store(0, first, _nn(grad_scores, b[:last]))
        dk = _tn(grad_scores, a[first:last])
        dv = _tn(probs.astype(jnp.bfloat16), g[first:last])
        if last == length:
            dk_ref[...] = dk
            dv_ref[...] = dv
        else:
            dk_ref[:last] += dk
            dv_ref[:last] += dv
    store(1, 0, dk_ref[...])
    store(2, 0, dv_ref[...])


HBM = pl.BlockSpec(memory_space=pltpu.HBM)
FULL = 60 * 2**20
PIECE = 128
SMALL = pl.CostEstimate(flops=1, bytes_accessed=1, transcendentals=0)


def _move(kernel, out_shape, inputs, n, name, in_specs=None, vmem=8 * 2**20):
    return pl.pallas_call(
        kernel,
        in_specs=in_specs or [HBM] * len(inputs),
        out_specs=HBM,
        out_shape=jax.ShapeDtypeStruct(out_shape, jnp.bfloat16),
        scratch_shapes=[
            pltpu.VMEM(out_shape, jnp.bfloat16),
            pltpu.SemaphoreType.DMA((n,)),
            pltpu.SemaphoreType.DMA((n,)),
        ],
        compiler_params=pltpu.CompilerParams(vmem_limit_bytes=vmem),
        cost_estimate=SMALL,
        name=name,
    )(*inputs)


def _through(pairs, buf_ref, out_ref, in_sems, out_sems):
    into = [
        pltpu.make_async_copy(src, buf_ref.at[place], in_sems.at[i]) for i, (src, place) in enumerate(pairs)
    ]
    out = [
        pltpu.make_async_copy(buf_ref.at[place], out_ref.at[place], out_sems.at[i])
        for i, (_, place) in enumerate(pairs)
    ]
    for copy in into:
        copy.start()
    for first, second in zip(into, out):
        first.wait()
        second.start()
    for copy in out:
        copy.wait()


def held_block(fetch_slot, stash_held):
    _, _, n, length, feat = stash_held.shape

    def kernel(slot_ref, stash_ref, out_ref, buf_ref, in_sems, out_sems):
        slot = slot_ref[lax.axis_size("pipe") - 1 - lax.axis_index("pipe")]
        _through([(stash_ref.at[0, slot, i], i) for i in range(n)], buf_ref, out_ref, in_sems, out_sems)

    specs = [pl.BlockSpec(memory_space=pltpu.SMEM), HBM]
    return _move(kernel, (n, length, feat), (fetch_slot, stash_held), n, "held_block", specs, FULL)


def pack_tokens(arrays, parts, after=()):
    n = len(arrays)
    _, rows, feat = arrays[0].shape
    own, some = feat // parts, rows // 2

    def kernel(*refs):
        out_ref, buf_ref, in_sems, out_sems = refs[-4:]
        pairs = [
            (refs[i].at[0, pl.ds(j * some, some), pl.ds(p * own, own)], (j, p, i))
            for j in range(2)
            for p in range(parts)
            for i in range(n)
        ]
        _through(pairs, buf_ref, out_ref, in_sems, out_sems)

    return _move(kernel, (2, parts, n, some, own), (*arrays, *after), 2 * parts * n, "pack_tokens", vmem=FULL)


def unpack_tokens(x):
    parts, n, rows, own = x.shape

    def kernel(x_ref, out_ref, buf_ref, in_sems, out_sems):
        pairs = [(x_ref.at[p, i], (i, slice(None), pl.ds(p * own, own))) for p in range(parts) for i in range(n)]
        _through(pairs, buf_ref, out_ref, in_sems, out_sems)

    return _move(kernel, (n, rows, parts * own), (x,), parts * n, "unpack_tokens")


def forward_core(x, rows_up):
    chunks, parts, _, rows, feat = x.shape
    part_rows = chunks * rows
    main = 3 * parts * part_rows - PIECE
    return pl.pallas_call(
        _forward_kernel,
        grid=(feat // HD,),
        in_specs=[
            pl.BlockSpec((chunks, parts, 3, rows, HD), lambda h: (0, 0, 0, 0, h)),
            pl.BlockSpec(rows_up.shape, lambda h: (0, 0, 0)),
        ],
        out_specs=[
            pl.BlockSpec((parts, 2, part_rows, HD), lambda h: (0, 0, 0, h)),
            pl.BlockSpec((main, HD), lambda h: (0, h)),
            pl.BlockSpec((PIECE, HD), lambda h: (0, h)),
        ],
        out_shape=[
            jax.ShapeDtypeStruct((parts, 2, part_rows, feat), jnp.bfloat16),
            jax.ShapeDtypeStruct((main, feat), jnp.bfloat16),
            jax.ShapeDtypeStruct((PIECE, feat), jnp.bfloat16),
        ],
        compiler_params=pltpu.CompilerParams(vmem_limit_bytes=24 * 2**20),
        cost_estimate=SMALL,
        name="forward_core",
    )(x, rows_up)


def backward_core(fetched, upstream, after):
    parts, rows, feat = upstream.shape
    length = parts * rows

    def kernel(f_ref, g_ref, _, *refs):
        _backward_kernel(f_ref, g_ref, *refs)

    return pl.pallas_call(
        kernel,
        grid=(feat // HD,),
        in_specs=[
            pl.BlockSpec((3, length, HD), lambda h: (0, 0, h)),
            pl.BlockSpec((parts, rows, HD), lambda h: (0, 0, h)),
            pl.BlockSpec(memory_space=pl.ANY),
        ],
        out_specs=pl.BlockSpec((parts, 3, rows, HD), lambda h: (0, 0, 0, h)),
        out_shape=jax.ShapeDtypeStruct((parts, 3, rows, feat), jnp.bfloat16),
        scratch_shapes=[pltpu.VMEM((length, HD), jnp.float32)] * 2,
        compiler_params=pltpu.CompilerParams(vmem_limit_bytes=24 * 2**20),
        cost_estimate=SMALL,
        name="backward_core",
    )(fetched, upstream, after)


def place(rows, shape, after):
    length = shape[2]
    starts = [k * PIECE for k in range(rows.shape[0] // PIECE)]

    def kernel(x_ref, *refs):
        out_ref, buf_ref, in_sems, out_sems = refs[-4:]
        into = [make_copy(x_ref, buf_ref, k, k, in_sems.at[i]) for i, k in enumerate(starts)]
        out = [
            pltpu.make_async_copy(
                buf_ref.at[pl.ds(k, PIECE)], out_ref.at[0, k // length, pl.ds(k % length, PIECE)], out_sems.at[i]
            )
            for i, k in enumerate(starts)
        ]
        for copy in into:
            copy.start()
        for first, second in zip(into, out):
            first.wait()
            second.start()
        for copy in out:
            copy.wait()

    def make_copy(src, dst, k, t, sem):
        return pltpu.make_async_copy(src.at[pl.ds(k, PIECE)], dst.at[pl.ds(t, PIECE)], sem)

    return pl.pallas_call(
        kernel,
        in_specs=[HBM] * (1 + len(after)),
        out_specs=HBM,
        out_shape=jax.ShapeDtypeStruct(shape, jnp.bfloat16),
        scratch_shapes=[
            pltpu.VMEM(rows.shape, jnp.bfloat16),
            pltpu.SemaphoreType.DMA((len(starts),)),
            pltpu.SemaphoreType.DMA((len(starts),)),
        ],
        compiler_params=pltpu.CompilerParams(vmem_limit_bytes=FULL),
        cost_estimate=SMALL,
        name="place",
    )(rows, *after)


def place_last(rows, out):
    n, length = out.shape[1:3]
    first = length - rows.shape[0]

    def kernel(x_ref, _, out_ref, sem):
        copy = pltpu.make_async_copy(x_ref, out_ref.at[0, n - 1, pl.ds(first, rows.shape[0])], sem)
        copy.start()
        copy.wait()

    return pl.pallas_call(
        kernel,
        in_specs=[pl.BlockSpec(memory_space=pltpu.VMEM), HBM],
        out_specs=HBM,
        out_shape=jax.ShapeDtypeStruct(out.shape, out.dtype),
        scratch_shapes=[pltpu.SemaphoreType.DMA],
        input_output_aliases={1: 0},
        compiler_params=pltpu.CompilerParams(vmem_limit_bytes=8 * 2**20),
        cost_estimate=SMALL,
        name="place_last",
    )(rows, out)


def exchange(x):
    return lax.all_to_all(x, "tensor", split_axis=0, concat_axis=0, tiled=True)


def on_device(query_new, key_new, value_new, stash_held, fetch_slot, cotangent):
    sections = lax.axis_size("pipe")
    section = lax.axis_index("pipe")
    parts = lax.axis_size("tensor")
    mirror = [(s, sections - 1 - s) for s in range(sections)]

    upstream = lax.ppermute(cotangent, "pipe", [(s, (s - 1) % sections) for s in range(sections)])
    held = held_block(fetch_slot, stash_held)
    fetched = lax.ppermute(held, "pipe", mirror)

    packed = pack_tokens((query_new, key_new, value_new), parts, after=(held,))
    output, block, last = forward_core(lax.map(exchange, packed), upstream)
    both = exchange(output)
    half = sections // 2
    crossing = lax.ppermute(both[:, 0], "pipe", [(half - 1, half)])

    steps = [(0, 2), (1, 3), (half - 2, half - 4), (half - 1, half - 3)]
    steps = steps + [(s + half, t + half) for s, t in steps]
    token, fetched = lax.optimization_barrier((cotangent[0, :16, :128], fetched))
    token = lax.ppermute(token, "pipe", steps)
    block, token, fetched = lax.optimization_barrier((block, token, fetched))
    moved = lax.ppermute(block, "pipe", mirror)
    last = lax.ppermute(last, "pipe", mirror)

    grads = backward_core(fetched, both[:, 1], token)
    grads, crossing = lax.optimization_barrier((grads, crossing))
    output, _ = lax.optimization_barrier((both[:, 0], token))
    output = lax.ppermute(output, "pipe", [(s, s + 1) for s in range(sections - 1) if s + 1 != half])
    output = jnp.where(lax.axis_index("pipe") == half, crossing, output)
    received = unpack_tokens(output[:, None])
    gradients = unpack_tokens(exchange(grads))[None]
    evicted = place(moved, (1, *held.shape), (received, gradients))
    return received, gradients, place_last(last, evicted)


def solution(mesh):
    in_specs = (
        P(("dp", "pipe"), "tensor", None),
        P(("dp", "pipe"), "tensor", None),
        P(("dp", "pipe"), "tensor", None),
        P(("dp", "pipe"), None, None, None, "tensor"),
        P("dp"),
        P(("dp", "pipe"), "tensor", None),
    )
    out_specs = (
        P(("dp", "pipe"), "tensor", None),
        P(("dp", "pipe"), None, "tensor", None),
        P(("dp", "pipe"), None, None, "tensor"),
    )
    return jax.shard_map(
        on_device, mesh=mesh, in_specs=in_specs, out_specs=out_specs, check_vma=False
    )
```

```python
import jax
import jax.numpy as jnp
from jax import lax
from jax.experimental import pallas as pl
from jax.experimental.pallas import tpu as pltpu
from jax.sharding import PartitionSpec as P

HD = 128
SCALE = HD ** (-0.5)
ROWS = 256


def _nt(a, b):
    return lax.dot_general(a, b, (((1,), (1,)), ((), ())), preferred_element_type=jnp.float32)


def _nn(a, b):
    return lax.dot_general(a, b, (((1,), (0,)), ((), ())), preferred_element_type=jnp.float32)


def _tn(a, b):
    return lax.dot_general(a, b, (((0,), (0,)), ((), ())), preferred_element_type=jnp.float32)


def _probs(a, b, first):
    scores = _nt(a, b) * SCALE
    row = lax.broadcasted_iota(jnp.int32, scores.shape, 0) + first
    col = lax.broadcasted_iota(jnp.int32, scores.shape, 1)
    scores = jnp.where(col <= row, scores, -1e30)
    shifted = jnp.exp(scores - jnp.max(scores, axis=-1, keepdims=True))
    return shifted / jnp.sum(shifted, axis=-1, keepdims=True)


def _forward_kernel(x_ref, u_ref, o_ref, b_ref, c_ref):
    parts, _, part_rows, _ = x_ref.shape
    length = parts * part_rows
    q, k, v = (x_ref[:, i].reshape(length, HD) for i in range(3))
    main = b_ref.shape[0] - 2 * length
    b_ref[:length] = q
    b_ref[length : 2 * length] = k
    b_ref[2 * length :] = v[:main]
    c_ref[...] = v[main:]
    feat = u_ref.shape[-1] // parts
    for p in range(parts):
        o_ref[p, 1] = u_ref[0, :, pl.ds(pl.multiple_of(p * feat + pl.program_id(0) * HD, HD), HD)]
    for first in range(0, length, ROWS):
        last = first + ROWS
        weights = _probs(q[first:last], k[:last], first).astype(jnp.bfloat16)
        out = _nn(weights, v[:last]).astype(jnp.bfloat16)
        o_ref[first // part_rows : last // part_rows, 0] = out.reshape(ROWS // part_rows, part_rows, HD)


def _backward_kernel(f_ref, g_ref, o_ref, dk_ref, dv_ref):
    parts, rows, _ = g_ref.shape
    length = parts * rows
    a, b, c = (f_ref[i] for i in range(3))
    g = g_ref[...].reshape(length, HD)

    def store(kind, first, x):
        x = x.astype(jnp.bfloat16).reshape(x.shape[0] // rows, rows, HD)
        o_ref[first // rows : first // rows + x.shape[0], kind] = x

    for first in reversed(range(0, length, ROWS)):
        last = first + ROWS
        probs = _probs(a[first:last], b[:last], first)
        grad_probs = _nt(g[first:last], c[:last])
        centre = jnp.sum(probs * grad_probs, axis=-1, keepdims=True)
        grad_scores = (probs * (grad_probs - centre) * SCALE).astype(jnp.bfloat16)
        store(0, first, _nn(grad_scores, b[:last]))
        dk = _tn(grad_scores, a[first:last])
        dv = _tn(probs.astype(jnp.bfloat16), g[first:last])
        if last == length:
            dk_ref[...] = dk
            dv_ref[...] = dv
        else:
            dk_ref[:last] += dk
            dv_ref[:last] += dv
    store(1, 0, dk_ref[...])
    store(2, 0, dv_ref[...])


HBM = pl.BlockSpec(memory_space=pltpu.HBM)
FULL = 60 * 2**20
PIECE = 128
SMALL = pl.CostEstimate(flops=1, bytes_accessed=1, transcendentals=0)


def _move(kernel, out_shape, inputs, n, name, in_specs=None, vmem=8 * 2**20):
    return pl.pallas_call(
        kernel,
        in_specs=in_specs or [HBM] * len(inputs),
        out_specs=HBM,
        out_shape=jax.ShapeDtypeStruct(out_shape, jnp.bfloat16),
        scratch_shapes=[
            pltpu.VMEM(out_shape, jnp.bfloat16),
            pltpu.SemaphoreType.DMA((n,)),
            pltpu.SemaphoreType.DMA((n,)),
        ],
        compiler_params=pltpu.CompilerParams(vmem_limit_bytes=vmem),
        cost_estimate=SMALL,
        name=name,
    )(*inputs)


def _through(pairs, buf_ref, out_ref, in_sems, out_sems):
    into = [
        pltpu.make_async_copy(src, buf_ref.at[place], in_sems.at[i]) for i, (src, place) in enumerate(pairs)
    ]
    out = [
        pltpu.make_async_copy(buf_ref.at[place], out_ref.at[place], out_sems.at[i])
        for i, (_, place) in enumerate(pairs)
    ]
    for copy in into:
        copy.start()
    for first, second in zip(into, out):
        first.wait()
        second.start()
    for copy in out:
        copy.wait()


def held_block(fetch_slot, stash_held):
    _, _, n, length, feat = stash_held.shape

    def kernel(slot_ref, stash_ref, out_ref, buf_ref, in_sems, out_sems):
        slot = slot_ref[lax.axis_size("pipe") - 1 - lax.axis_index("pipe")]
        _through([(stash_ref.at[0, slot, i], i) for i in range(n)], buf_ref, out_ref, in_sems, out_sems)

    specs = [pl.BlockSpec(memory_space=pltpu.SMEM), HBM]
    return _move(kernel, (n, length, feat), (fetch_slot, stash_held), n, "held_block", specs, FULL)


def pack_tokens(arrays, parts, after=()):
    n = len(arrays)
    _, rows, feat = arrays[0].shape
    own = feat // parts

    def kernel(*refs):
        out_ref, buf_ref, in_sems, out_sems = refs[-4:]
        pairs = [(refs[i].at[0, :, pl.ds(p * own, own)], (p, i)) for p in range(parts) for i in range(n)]
        _through(pairs, buf_ref, out_ref, in_sems, out_sems)

    return _move(kernel, (parts, n, rows, own), (*arrays, *after), parts * n, "pack_tokens", vmem=FULL)


def unpack_tokens(x):
    parts, n, rows, own = x.shape

    def kernel(x_ref, out_ref, buf_ref, in_sems, out_sems):
        pairs = [(x_ref.at[p, i], (i, slice(None), pl.ds(p * own, own))) for p in range(parts) for i in range(n)]
        _through(pairs, buf_ref, out_ref, in_sems, out_sems)

    return _move(kernel, (n, rows, parts * own), (x,), parts * n, "unpack_tokens")


def forward_core(x, rows_up):
    parts, _, part_rows, feat = x.shape
    main = 3 * parts * part_rows - PIECE
    return pl.pallas_call(
        _forward_kernel,
        grid=(feat // HD,),
        in_specs=[
            pl.BlockSpec((parts, 3, part_rows, HD), lambda h: (0, 0, 0, h)),
            pl.BlockSpec(rows_up.shape, lambda h: (0, 0, 0)),
        ],
        out_specs=[
            pl.BlockSpec((parts, 2, part_rows, HD), lambda h: (0, 0, 0, h)),
            pl.BlockSpec((main, HD), lambda h: (0, h)),
            pl.BlockSpec((PIECE, HD), lambda h: (0, h)),
        ],
        out_shape=[
            jax.ShapeDtypeStruct((parts, 2, part_rows, feat), jnp.bfloat16),
            jax.ShapeDtypeStruct((main, feat), jnp.bfloat16),
            jax.ShapeDtypeStruct((PIECE, feat), jnp.bfloat16),
        ],
        compiler_params=pltpu.CompilerParams(vmem_limit_bytes=24 * 2**20),
        cost_estimate=pl.CostEstimate(flops=23000000000, bytes_accessed=73800000, transcendentals=0),
        name="forward_core",
    )(x, rows_up)


def backward_core(fetched, upstream):
    parts, rows, feat = upstream.shape
    length = parts * rows

    return pl.pallas_call(
        _backward_kernel,
        grid=(feat // HD,),
        in_specs=[
            pl.BlockSpec((3, length, HD), lambda h: (0, 0, h)),
            pl.BlockSpec((parts, rows, HD), lambda h: (0, 0, h)),
        ],
        out_specs=pl.BlockSpec((parts, 3, rows, HD), lambda h: (0, 0, 0, h)),
        out_shape=jax.ShapeDtypeStruct((parts, 3, rows, feat), jnp.bfloat16),
        scratch_shapes=[pltpu.VMEM((length, HD), jnp.float32)] * 2,
        compiler_params=pltpu.CompilerParams(vmem_limit_bytes=24 * 2**20),
        cost_estimate=SMALL,
        name="backward_core",
    )(fetched, upstream)


def place(rows, shape, after):
    length = shape[2]
    starts = [k * PIECE for k in range(rows.shape[0] // PIECE)]

    def kernel(x_ref, *refs):
        out_ref, buf_ref, in_sems, out_sems = refs[-4:]
        into = [make_copy(x_ref, buf_ref, k, k, in_sems.at[i]) for i, k in enumerate(starts)]
        out = [
            pltpu.make_async_copy(
                buf_ref.at[pl.ds(k, PIECE)], out_ref.at[0, k // length, pl.ds(k % length, PIECE)], out_sems.at[i]
            )
            for i, k in enumerate(starts)
        ]
        for copy in into:
            copy.start()
        for first, second in zip(into, out):
            first.wait()
            second.start()
        for copy in out:
            copy.wait()

    def make_copy(src, dst, k, t, sem):
        return pltpu.make_async_copy(src.at[pl.ds(k, PIECE)], dst.at[pl.ds(t, PIECE)], sem)

    return pl.pallas_call(
        kernel,
        in_specs=[HBM] * (1 + len(after)),
        out_specs=HBM,
        out_shape=jax.ShapeDtypeStruct(shape, jnp.bfloat16),
        scratch_shapes=[
            pltpu.VMEM(rows.shape, jnp.bfloat16),
            pltpu.SemaphoreType.DMA((len(starts),)),
            pltpu.SemaphoreType.DMA((len(starts),)),
        ],
        compiler_params=pltpu.CompilerParams(vmem_limit_bytes=FULL),
        cost_estimate=SMALL,
        name="place",
    )(rows, *after)


def place_last(rows, out):
    n, length = out.shape[1:3]
    first = length - rows.shape[0]

    def kernel(x_ref, _, out_ref, sem):
        copy = pltpu.make_async_copy(x_ref, out_ref.at[0, n - 1, pl.ds(first, rows.shape[0])], sem)
        copy.start()
        copy.wait()

    return pl.pallas_call(
        kernel,
        in_specs=[pl.BlockSpec(memory_space=pltpu.VMEM), HBM],
        out_specs=HBM,
        out_shape=jax.ShapeDtypeStruct(out.shape, out.dtype),
        scratch_shapes=[pltpu.SemaphoreType.DMA],
        input_output_aliases={1: 0},
        compiler_params=pltpu.CompilerParams(vmem_limit_bytes=8 * 2**20),
        cost_estimate=SMALL,
        name="place_last",
    )(rows, out)


def exchange(x):
    return lax.all_to_all(x, "tensor", split_axis=0, concat_axis=0, tiled=True)


def apart(x, times):
    def step(state):
        return state[0] + 1, exchange(state[1])

    return lax.while_loop(lambda state: state[0] < times, step, (0, x))[1]


def on_device(query_new, key_new, value_new, stash_held, fetch_slot, cotangent):
    sections = lax.axis_size("pipe")
    section = lax.axis_index("pipe")
    parts = lax.axis_size("tensor")
    mirror = [(s, sections - 1 - s) for s in range(sections)]

    once = jnp.minimum(jnp.max(fetch_slot) + 1, 1)
    upstream = lax.ppermute(cotangent, "pipe", [(s, (s - 1) % sections) for s in range(sections)])
    held = held_block(fetch_slot, stash_held)
    fetched = lax.ppermute(held, "pipe", mirror)

    packed = pack_tokens((query_new, key_new, value_new), parts, after=(held,))
    output, block, last = forward_core(apart(packed, once), upstream)
    both = apart(output, once)
    output = lax.ppermute(both[:, 0], "pipe", [(s, s + 1) for s in range(sections - 1)])

    block, both = lax.optimization_barrier((block, both))
    moved = lax.ppermute(block, "pipe", mirror)
    last = lax.ppermute(last, "pipe", mirror)

    grads = backward_core(fetched, both[:, 1])
    grads, output = lax.optimization_barrier((grads, output))
    received = unpack_tokens(output[:, None])
    gradients = unpack_tokens(exchange(grads))[None]
    evicted = place(moved, (1, *held.shape), (received, gradients))
    return received, gradients, place_last(last, evicted)


def solution(mesh):
    in_specs = (
        P(("dp", "pipe"), "tensor", None),
        P(("dp", "pipe"), "tensor", None),
        P(("dp", "pipe"), "tensor", None),
        P(("dp", "pipe"), None, None, None, "tensor"),
        P("dp"),
        P(("dp", "pipe"), "tensor", None),
    )
    out_specs = (
        P(("dp", "pipe"), "tensor", None),
        P(("dp", "pipe"), None, "tensor", None),
        P(("dp", "pipe"), None, None, "tensor"),
    )
    return jax.shard_map(
        on_device, mesh=mesh, in_specs=in_specs, out_specs=out_specs, check_vma=False
    )
```

```python
import jax
import jax.numpy as jnp
from jax import lax
from jax.experimental import pallas as pl
from jax.experimental.pallas import tpu as pltpu
from jax.sharding import PartitionSpec as P

HD = 128
SCALE = HD ** (-0.5)
ROWS = 256


def _nt(a, b):
    return lax.dot_general(a, b, (((1,), (1,)), ((), ())), preferred_element_type=jnp.float32)


def _nn(a, b):
    return lax.dot_general(a, b, (((1,), (0,)), ((), ())), preferred_element_type=jnp.float32)


def _tn(a, b):
    return lax.dot_general(a, b, (((0,), (0,)), ((), ())), preferred_element_type=jnp.float32)


def _probs(a, b, first):
    scores = _nt(a, b) * SCALE
    row = lax.broadcasted_iota(jnp.int32, scores.shape, 0) + first
    col = lax.broadcasted_iota(jnp.int32, scores.shape, 1)
    scores = jnp.where(col <= row, scores, -1e30)
    shifted = jnp.exp(scores - jnp.max(scores, axis=-1, keepdims=True))
    return shifted / jnp.sum(shifted, axis=-1, keepdims=True)


def _forward_kernel(x_ref, o_ref, b_ref, c_ref):
    parts, _, part_rows, _ = x_ref.shape
    length = parts * part_rows
    q, k, v = (x_ref[:, i].reshape(length, HD) for i in range(3))
    main = b_ref.shape[0] - 2 * length
    b_ref[:length] = q
    b_ref[length : 2 * length] = k
    b_ref[2 * length :] = v[:main]
    c_ref[...] = v[main:]
    for first in range(0, length, ROWS):
        last = first + ROWS
        weights = _probs(q[first:last], k[:last], first).astype(jnp.bfloat16)
        out = _nn(weights, v[:last]).astype(jnp.bfloat16)
        o_ref[first // part_rows : last // part_rows, 0] = out.reshape(ROWS // part_rows, part_rows, HD)


def _backward_kernel(f_ref, g_ref, o_ref, dk_ref, dv_ref):
    parts, rows, _ = g_ref.shape
    length = parts * rows
    a, b, c = (f_ref[i * length : (i + 1) * length] for i in range(3))
    g = g_ref[...].reshape(length, HD)

    def store(kind, first, x):
        x = x.astype(jnp.bfloat16).reshape(x.shape[0] // rows, rows, HD)
        o_ref[first // rows : first // rows + x.shape[0], kind] = x

    for first in reversed(range(0, length, ROWS)):
        last = first + ROWS
        probs = _probs(a[first:last], b[:last], first)
        grad_probs = _nt(g[first:last], c[:last])
        centre = jnp.sum(probs * grad_probs, axis=-1, keepdims=True)
        grad_scores = (probs * (grad_probs - centre) * SCALE).astype(jnp.bfloat16)
        store(0, first, _nn(grad_scores, b[:last]))
        dk = _tn(grad_scores, a[first:last])
        dv = _tn(probs.astype(jnp.bfloat16), g[first:last])
        if last == length:
            dk_ref[...] = dk
            dv_ref[...] = dv
        else:
            dk_ref[:last] += dk
            dv_ref[:last] += dv
    store(1, 0, dk_ref[...])
    store(2, 0, dv_ref[...])


HBM = pl.BlockSpec(memory_space=pltpu.HBM)
FULL = 60 * 2**20
PIECE = 128
AROUND = 256
SMALL = pl.CostEstimate(flops=1, bytes_accessed=1, transcendentals=0)


def _move(kernel, out_shape, inputs, n, name, in_specs=None, vmem=8 * 2**20):
    return pl.pallas_call(
        kernel,
        in_specs=in_specs or [HBM] * len(inputs),
        out_specs=HBM,
        out_shape=jax.ShapeDtypeStruct(out_shape, jnp.bfloat16),
        scratch_shapes=[
            pltpu.VMEM(out_shape, jnp.bfloat16),
            pltpu.SemaphoreType.DMA((n,)),
            pltpu.SemaphoreType.DMA((n,)),
        ],
        compiler_params=pltpu.CompilerParams(vmem_limit_bytes=vmem),
        cost_estimate=SMALL,
        name=name,
    )(*inputs)


def _through(pairs, buf_ref, out_ref, in_sems, out_sems):
    into = [
        pltpu.make_async_copy(src, buf_ref.at[place], in_sems.at[i]) for i, (src, place) in enumerate(pairs)
    ]
    out = [
        pltpu.make_async_copy(buf_ref.at[place], out_ref.at[place], out_sems.at[i])
        for i, (_, place) in enumerate(pairs)
    ]
    for copy in into:
        copy.start()
    for first, second in zip(into, out):
        first.wait()
        second.start()
    for copy in out:
        copy.wait()


def held_block(fetch_slot, stash_held):
    _, _, n, length, feat = stash_held.shape

    def kernel(slot_ref, stash_ref, out_ref, end_ref, buf_ref, in_sems, out_sems):
        slot = slot_ref[lax.axis_size("pipe") - 1 - lax.axis_index("pipe")]
        into = [pltpu.make_async_copy(stash_ref.at[0, slot, i], buf_ref.at[i], in_sems.at[i]) for i in range(n)]
        out = [pltpu.make_async_copy(buf_ref.at[i], out_ref.at[i], out_sems.at[i]) for i in range(n)]
        last = pltpu.make_async_copy(buf_ref.at[n - 1, pl.ds(length - AROUND, AROUND)], end_ref, out_sems.at[n])
        for copy in into:
            copy.start()
        for first, second in zip(into, out):
            first.wait()
            second.start()
        last.start()
        for copy in (*out, last):
            copy.wait()

    return pl.pallas_call(
        kernel,
        in_specs=[pl.BlockSpec(memory_space=pltpu.SMEM), HBM],
        out_specs=[HBM, HBM],
        out_shape=[
            jax.ShapeDtypeStruct((n, length, feat), jnp.bfloat16),
            jax.ShapeDtypeStruct((AROUND, feat), jnp.bfloat16),
        ],
        scratch_shapes=[
            pltpu.VMEM((n, length, feat), jnp.bfloat16),
            pltpu.SemaphoreType.DMA((n,)),
            pltpu.SemaphoreType.DMA((n + 1,)),
        ],
        compiler_params=pltpu.CompilerParams(vmem_limit_bytes=FULL),
        cost_estimate=SMALL,
        name="held_block",
    )(fetch_slot, stash_held)


def pack_tokens(arrays, parts, after=()):
    n = len(arrays)
    _, rows, feat = arrays[0].shape
    own = feat // parts

    def kernel(*refs):
        out_ref, buf_ref, in_sems, out_sems = refs[-4:]
        pairs = [(refs[i].at[0, :, pl.ds(p * own, own)], (p, i)) for p in range(parts) for i in range(n)]
        _through(pairs, buf_ref, out_ref, in_sems, out_sems)

    return _move(kernel, (parts, n, rows, own), (*arrays, *after), parts * n, "pack_tokens", vmem=FULL)


def unpack_tokens(x):
    parts, n, rows, own = x.shape

    def kernel(x_ref, out_ref, buf_ref, in_sems, out_sems):
        pairs = [(x_ref.at[p, i], (i, slice(None), pl.ds(p * own, own))) for p in range(parts) for i in range(n)]
        _through(pairs, buf_ref, out_ref, in_sems, out_sems)

    return _move(kernel, (n, rows, parts * own), (x,), parts * n, "unpack_tokens")


def pack_beside(x, rows_up):
    parts, _, rows, own = x.shape

    def kernel(_, up_ref, out_ref, buf_ref, in_sems, out_sems):
        pairs = [(up_ref.at[0, :, pl.ds(p * own, own)], p) for p in range(parts)]
        _through(pairs, buf_ref, out_ref.at[:, 1], in_sems, out_sems)

    return pl.pallas_call(
        kernel,
        in_specs=[HBM] * 2,
        out_specs=HBM,
        out_shape=jax.ShapeDtypeStruct(x.shape, x.dtype),
        scratch_shapes=[
            pltpu.VMEM((parts, rows, own), jnp.bfloat16),
            pltpu.SemaphoreType.DMA((parts,)),
            pltpu.SemaphoreType.DMA((parts,)),
        ],
        input_output_aliases={0: 0},
        compiler_params=pltpu.CompilerParams(vmem_limit_bytes=FULL),
        cost_estimate=pl.CostEstimate(flops=23000000000, bytes_accessed=73800000, transcendentals=0),
        name="pack_beside",
    )(x, rows_up)


def forward_core(x):
    parts, _, part_rows, feat = x.shape
    main = 3 * parts * part_rows - PIECE
    return pl.pallas_call(
        _forward_kernel,
        grid=(feat // HD,),
        in_specs=[
            pl.BlockSpec((parts, 3, part_rows, HD), lambda h: (0, 0, 0, h)),
        ],
        out_specs=[
            pl.BlockSpec((parts, 1, part_rows, HD), lambda h: (0, 0, 0, h)),
            pl.BlockSpec((main, HD), lambda h: (0, h)),
            pl.BlockSpec((PIECE, HD), lambda h: (0, h)),
        ],
        out_shape=[
            jax.ShapeDtypeStruct((parts, 2, part_rows, feat), jnp.bfloat16),
            jax.ShapeDtypeStruct((main, feat), jnp.bfloat16),
            jax.ShapeDtypeStruct((PIECE, feat), jnp.bfloat16),
        ],
        compiler_params=pltpu.CompilerParams(vmem_limit_bytes=24 * 2**20),
        cost_estimate=SMALL,
        name="forward_core",
    )(x)


def one_of(index, members):
    found = index == members[0]
    for m in members[1:]:
        found = found | (index == m)
    return found


def backward_core(whole, main, end, upstream, in_two):
    parts, rows, feat = upstream.shape
    length = parts * rows

    def kernel(w_ref, m_ref, e_ref, g_ref, o_ref, f_ref, dk_ref, dv_ref):
        here = one_of(lax.axis_index("pipe"), in_two)
        first = m_ref.shape[0]

        @pl.when(here)
        def _():
            f_ref[:first] = m_ref[...]
            f_ref[first:] = e_ref[...]

        @pl.when(jnp.logical_not(here))
        def _():
            f_ref[...] = w_ref[...]

        _backward_kernel(f_ref, g_ref, o_ref, dk_ref, dv_ref)

    return pl.pallas_call(
        kernel,
        grid=(feat // HD,),
        in_specs=[pl.BlockSpec((x.shape[0], HD), lambda h: (0, h)) for x in (whole, main, end)]
        + [pl.BlockSpec((parts, rows, HD), lambda h: (0, 0, h))],
        out_specs=pl.BlockSpec((parts, 3, rows, HD), lambda h: (0, 0, 0, h)),
        out_shape=jax.ShapeDtypeStruct((parts, 3, rows, feat), jnp.bfloat16),
        scratch_shapes=[pltpu.VMEM((3 * length, HD), jnp.bfloat16)] + [pltpu.VMEM((length, HD), jnp.float32)] * 2,
        compiler_params=pltpu.CompilerParams(vmem_limit_bytes=24 * 2**20),
        cost_estimate=SMALL,
        name="backward_core",
    )(whole, main, end, upstream)


def place(rows, shape, after):
    length = shape[2]
    starts = [k * PIECE for k in range(rows.shape[0] // PIECE)]

    def kernel(x_ref, *refs):
        out_ref, buf_ref, in_sems, out_sems = refs[-4:]
        into = [make_copy(x_ref, buf_ref, k, k, in_sems.at[i]) for i, k in enumerate(starts)]
        out = [
            pltpu.make_async_copy(
                buf_ref.at[pl.ds(k, PIECE)], out_ref.at[0, k // length, pl.ds(k % length, PIECE)], out_sems.at[i]
            )
            for i, k in enumerate(starts)
        ]
        for copy in into:
            copy.start()
        for first, second in zip(into, out):
            first.wait()
            second.start()
        for copy in out:
            copy.wait()

    def make_copy(src, dst, k, t, sem):
        return pltpu.make_async_copy(src.at[pl.ds(k, PIECE)], dst.at[pl.ds(t, PIECE)], sem)

    return pl.pallas_call(
        kernel,
        in_specs=[HBM] * (1 + len(after)),
        out_specs=HBM,
        out_shape=jax.ShapeDtypeStruct(shape, jnp.bfloat16),
        scratch_shapes=[
            pltpu.VMEM(rows.shape, jnp.bfloat16),
            pltpu.SemaphoreType.DMA((len(starts),)),
            pltpu.SemaphoreType.DMA((len(starts),)),
        ],
        compiler_params=pltpu.CompilerParams(vmem_limit_bytes=FULL),
        cost_estimate=SMALL,
        name="place",
    )(rows, *after)


def place_last(rows, out):
    n, length = out.shape[1:3]
    first = length - rows.shape[0]

    def kernel(x_ref, _, out_ref, sem):
        copy = pltpu.make_async_copy(x_ref, out_ref.at[0, n - 1, pl.ds(first, rows.shape[0])], sem)
        copy.start()
        copy.wait()

    return pl.pallas_call(
        kernel,
        in_specs=[pl.BlockSpec(memory_space=pltpu.VMEM), HBM],
        out_specs=HBM,
        out_shape=jax.ShapeDtypeStruct(out.shape, out.dtype),
        scratch_shapes=[pltpu.SemaphoreType.DMA],
        input_output_aliases={1: 0},
        compiler_params=pltpu.CompilerParams(vmem_limit_bytes=8 * 2**20),
        cost_estimate=SMALL,
        name="place_last",
    )(rows, out)


def exchange(x):
    return lax.all_to_all(x, "tensor", split_axis=0, concat_axis=0, tiled=True)


def apart(x, times):
    def step(state):
        return state[0] + 1, exchange(state[1])

    return lax.while_loop(lambda state: state[0] < times, step, (0, x))[1]


def on_device(query_new, key_new, value_new, stash_held, fetch_slot, cotangent):
    sections = lax.axis_size("pipe")
    section = lax.axis_index("pipe")
    parts = lax.axis_size("tensor")
    mirror = [(s, sections - 1 - s) for s in range(sections)]

    once = jnp.minimum(jnp.max(fetch_slot) + 1, 1)
    upstream = lax.ppermute(cotangent, "pipe", [(s, (s - 1) % sections) for s in range(sections)])
    held, end = held_block(fetch_slot, stash_held)
    half = sections // 2
    shared = [half - 3, half + 2, 2]
    beside = [(s, s ^ 1) for s in shared]
    end = lax.ppermute(end, "pipe", beside)
    end = lax.ppermute(end, "pipe", [(t, sections - 1 - s) for s, t in beside])
    rows_held = held.reshape(-1, held.shape[2])
    whole = lax.ppermute(rows_held, "pipe", [(s, t) for s, t in mirror if s not in shared])
    main = lax.ppermute(rows_held[:-AROUND], "pipe", [(s, t) for s, t in mirror if s in shared])

    packed = pack_tokens((query_new, key_new, value_new), parts, after=(held,))
    output, block, last = forward_core(apart(packed, once))
    both = apart(pack_beside(output, upstream), once)
    output = lax.ppermute(both[:, 0], "pipe", [(s, s + 1) for s in range(sections - 1)])

    block, both = lax.optimization_barrier((block, both))
    moved = lax.ppermute(block, "pipe", mirror)
    last = lax.ppermute(last, "pipe", mirror)

    grads = backward_core(whole, main, end, both[:, 1], [sections - 1 - s for s in shared])
    grads, output = lax.optimization_barrier((grads, output))
    received = unpack_tokens(output[:, None])
    gradients = unpack_tokens(exchange(grads))[None]
    evicted = place(moved, (1, *held.shape), (received, gradients))
    return received, gradients, place_last(last, evicted)


def solution(mesh):
    in_specs = (
        P(("dp", "pipe"), "tensor", None),
        P(("dp", "pipe"), "tensor", None),
        P(("dp", "pipe"), "tensor", None),
        P(("dp", "pipe"), None, None, None, "tensor"),
        P("dp"),
        P(("dp", "pipe"), "tensor", None),
    )
    out_specs = (
        P(("dp", "pipe"), "tensor", None),
        P(("dp", "pipe"), None, "tensor", None),
        P(("dp", "pipe"), None, None, "tensor"),
    )
    return jax.shard_map(
        on_device, mesh=mesh, in_specs=in_specs, out_specs=out_specs, check_vma=False
    )
```

```python
import jax
import jax.numpy as jnp
from jax import lax
from jax.experimental import pallas as pl
from jax.experimental.pallas import tpu as pltpu
from jax.sharding import PartitionSpec as P

HD = 128
SCALE = HD ** (-0.5)
ROWS = 256


def _nt(a, b):
    return lax.dot_general(a, b, (((1,), (1,)), ((), ())), preferred_element_type=jnp.float32)


def _nn(a, b):
    return lax.dot_general(a, b, (((1,), (0,)), ((), ())), preferred_element_type=jnp.float32)


def _tn(a, b):
    return lax.dot_general(a, b, (((0,), (0,)), ((), ())), preferred_element_type=jnp.float32)


def _probs(a, b, first):
    scores = _nt(a, b) * SCALE
    row = lax.broadcasted_iota(jnp.int32, scores.shape, 0) + first
    col = lax.broadcasted_iota(jnp.int32, scores.shape, 1)
    scores = jnp.where(col <= row, scores, -1e30)
    shifted = jnp.exp(scores - jnp.max(scores, axis=-1, keepdims=True))
    return shifted / jnp.sum(shifted, axis=-1, keepdims=True)


def _forward_kernel(x_ref, o_ref, b_ref, c_ref):
    parts, _, part_rows, _ = x_ref.shape
    length = parts * part_rows
    q, k, v = (x_ref[:, i].reshape(length, HD) for i in range(3))
    main = b_ref.shape[0] - 2 * length
    b_ref[:length] = q
    b_ref[length : 2 * length] = k
    b_ref[2 * length :] = v[:main]
    c_ref[...] = v[main:]
    for first in range(0, length, ROWS):
        last = first + ROWS
        weights = _probs(q[first:last], k[:last], first).astype(jnp.bfloat16)
        out = _nn(weights, v[:last]).astype(jnp.bfloat16)
        o_ref[first // part_rows : last // part_rows, 0] = out.reshape(ROWS // part_rows, part_rows, HD)


def _backward_kernel(f_ref, g_ref, o_ref, dk_ref, dv_ref):
    parts, rows, _ = g_ref.shape
    length = parts * rows
    a, b, c = (f_ref[i * length : (i + 1) * length] for i in range(3))
    g = g_ref[...].reshape(length, HD)

    def store(kind, first, x):
        x = x.astype(jnp.bfloat16).reshape(x.shape[0] // rows, rows, HD)
        o_ref[first // rows : first // rows + x.shape[0], kind] = x

    for first in reversed(range(0, length, ROWS)):
        last = first + ROWS
        probs = _probs(a[first:last], b[:last], first)
        grad_probs = _nt(g[first:last], c[:last])
        centre = jnp.sum(probs * grad_probs, axis=-1, keepdims=True)
        grad_scores = (probs * (grad_probs - centre) * SCALE).astype(jnp.bfloat16)
        store(0, first, _nn(grad_scores, b[:last]))
        dk = _tn(grad_scores, a[first:last])
        dv = _tn(probs.astype(jnp.bfloat16), g[first:last])
        if last == length:
            dk_ref[...] = dk
            dv_ref[...] = dv
        else:
            dk_ref[:last] += dk
            dv_ref[:last] += dv
    store(1, 0, dk_ref[...])
    store(2, 0, dv_ref[...])


HBM = pl.BlockSpec(memory_space=pltpu.HBM)
FULL = 60 * 2**20
PIECE = 128
AROUND = 256
SMALL = pl.CostEstimate(flops=1, bytes_accessed=1, transcendentals=0)


def _move(kernel, out_shape, inputs, n, name, in_specs=None, vmem=8 * 2**20):
    return pl.pallas_call(
        kernel,
        in_specs=in_specs or [HBM] * len(inputs),
        out_specs=HBM,
        out_shape=jax.ShapeDtypeStruct(out_shape, jnp.bfloat16),
        scratch_shapes=[
            pltpu.VMEM(out_shape, jnp.bfloat16),
            pltpu.SemaphoreType.DMA((n,)),
            pltpu.SemaphoreType.DMA((n,)),
        ],
        compiler_params=pltpu.CompilerParams(vmem_limit_bytes=vmem),
        cost_estimate=SMALL,
        name=name,
    )(*inputs)


def _through(pairs, buf_ref, out_ref, in_sems, out_sems):
    into = [
        pltpu.make_async_copy(src, buf_ref.at[place], in_sems.at[i]) for i, (src, place) in enumerate(pairs)
    ]
    out = [
        pltpu.make_async_copy(buf_ref.at[place], out_ref.at[place], out_sems.at[i])
        for i, (_, place) in enumerate(pairs)
    ]
    for copy in into:
        copy.start()
    for first, second in zip(into, out):
        first.wait()
        second.start()
    for copy in out:
        copy.wait()


def held_block(fetch_slot, stash_held, in_two):
    _, _, n, length, feat = stash_held.shape
    rows = n * length

    def kernel(slot_ref, stash_ref, whole_ref, main_ref, end_ref, buf_ref, in_sems, out_sems):
        section = lax.axis_index("pipe")
        slot = slot_ref[lax.axis_size("pipe") - 1 - section]
        here = one_of(section, in_two)

        def copy(first, size, dst, place, sem):
            return pltpu.make_async_copy(buf_ref.at[pl.ds(first, size)], dst.at[pl.ds(place, size)], out_sems.at[sem])

        into = [
            pltpu.make_async_copy(stash_ref.at[0, slot, i], buf_ref.at[pl.ds(i * length, length)], in_sems.at[i])
            for i in range(n)
        ]
        whole = [copy(i * length, length, whole_ref, i * length, i) for i in range(n)]
        main = [copy(i * length, length, main_ref, i * length, i) for i in range(n - 1)]
        main.append(copy((n - 1) * length, length - AROUND, main_ref, (n - 1) * length, n - 1))
        last = copy(rows - AROUND, AROUND, end_ref, 0, n)
        for c in into:
            c.start()

        @pl.when(here)
        def _():
            for first, second in zip(into, main):
                first.wait()
                second.start()
            last.start()
            for c in (*main, last):
                c.wait()

        @pl.when(jnp.logical_not(here))
        def _():
            for first, second in zip(into, whole):
                first.wait()
                second.start()
            for c in whole:
                c.wait()

    return pl.pallas_call(
        kernel,
        in_specs=[pl.BlockSpec(memory_space=pltpu.SMEM), HBM],
        out_specs=[HBM, HBM, HBM],
        out_shape=[jax.ShapeDtypeStruct((k, feat), jnp.bfloat16) for k in (rows, rows - AROUND, AROUND)],
        scratch_shapes=[
            pltpu.VMEM((rows, feat), jnp.bfloat16),
            pltpu.SemaphoreType.DMA((n,)),
            pltpu.SemaphoreType.DMA((n + 1,)),
        ],
        compiler_params=pltpu.CompilerParams(vmem_limit_bytes=FULL),
        cost_estimate=SMALL,
        name="held_block",
    )(fetch_slot, stash_held)


def pack_tokens(arrays, parts, after=()):
    n = len(arrays)
    _, rows, feat = arrays[0].shape
    own = feat // parts

    def kernel(*refs):
        out_ref, buf_ref, in_sems, out_sems = refs[-4:]
        pairs = [(refs[i].at[0, :, pl.ds(p * own, own)], (p, i)) for p in range(parts) for i in range(n)]
        _through(pairs, buf_ref, out_ref, in_sems, out_sems)

    return _move(kernel, (parts, n, rows, own), (*arrays, *after), parts * n, "pack_tokens", vmem=FULL)


def unpack_tokens(x):
    parts, n, rows, own = x.shape

    def kernel(x_ref, out_ref, buf_ref, in_sems, out_sems):
        pairs = [(x_ref.at[p, i], (i, slice(None), pl.ds(p * own, own))) for p in range(parts) for i in range(n)]
        _through(pairs, buf_ref, out_ref, in_sems, out_sems)

    return _move(kernel, (n, rows, parts * own), (x,), parts * n, "unpack_tokens")


def pack_beside(x, rows_up):
    parts, _, rows, own = x.shape

    def kernel(_, up_ref, out_ref, buf_ref, in_sems, out_sems):
        pairs = [(up_ref.at[0, :, pl.ds(p * own, own)], p) for p in range(parts)]
        _through(pairs, buf_ref, out_ref.at[:, 1], in_sems, out_sems)

    return pl.pallas_call(
        kernel,
        in_specs=[HBM] * 2,
        out_specs=HBM,
        out_shape=jax.ShapeDtypeStruct(x.shape, x.dtype),
        scratch_shapes=[
            pltpu.VMEM((parts, rows, own), jnp.bfloat16),
            pltpu.SemaphoreType.DMA((parts,)),
            pltpu.SemaphoreType.DMA((parts,)),
        ],
        input_output_aliases={0: 0},
        compiler_params=pltpu.CompilerParams(vmem_limit_bytes=FULL),
        cost_estimate=pl.CostEstimate(flops=23000000000, bytes_accessed=73800000, transcendentals=0),
        name="pack_beside",
    )(x, rows_up)


def forward_core(x):
    parts, _, part_rows, feat = x.shape
    main = 3 * parts * part_rows - PIECE
    return pl.pallas_call(
        _forward_kernel,
        grid=(feat // HD,),
        in_specs=[
            pl.BlockSpec((parts, 3, part_rows, HD), lambda h: (0, 0, 0, h)),
        ],
        out_specs=[
            pl.BlockSpec((parts, 1, part_rows, HD), lambda h: (0, 0, 0, h)),
            pl.BlockSpec((main, HD), lambda h: (0, h)),
            pl.BlockSpec((PIECE, HD), lambda h: (0, h)),
        ],
        out_shape=[
            jax.ShapeDtypeStruct((parts, 2, part_rows, feat), jnp.bfloat16),
            jax.ShapeDtypeStruct((main, feat), jnp.bfloat16),
            jax.ShapeDtypeStruct((PIECE, feat), jnp.bfloat16),
        ],
        compiler_params=pltpu.CompilerParams(vmem_limit_bytes=FULL),
        cost_estimate=SMALL,
        name="forward_core",
    )(x)


def one_of(index, members):
    found = index == members[0]
    for m in members[1:]:
        found = found | (index == m)
    return found


def backward_core(whole, main, end, upstream, in_two):
    parts, rows, feat = upstream.shape
    length = parts * rows

    def kernel(w_ref, m_ref, e_ref, g_ref, o_ref, f_ref, dk_ref, dv_ref):
        here = one_of(lax.axis_index("pipe"), in_two)
        first = m_ref.shape[0]

        @pl.when(here)
        def _():
            f_ref[:first] = m_ref[...]
            f_ref[first:] = e_ref[...]

        @pl.when(jnp.logical_not(here))
        def _():
            f_ref[...] = w_ref[...]

        _backward_kernel(f_ref, g_ref, o_ref, dk_ref, dv_ref)

    return pl.pallas_call(
        kernel,
        grid=(feat // HD,),
        in_specs=[pl.BlockSpec((x.shape[0], HD), lambda h: (0, h)) for x in (whole, main, end)]
        + [pl.BlockSpec((parts, rows, HD), lambda h: (0, 0, h))],
        out_specs=pl.BlockSpec((parts, 3, rows, HD), lambda h: (0, 0, 0, h)),
        out_shape=jax.ShapeDtypeStruct((parts, 3, rows, feat), jnp.bfloat16),
        scratch_shapes=[pltpu.VMEM((3 * length, HD), jnp.bfloat16)] + [pltpu.VMEM((length, HD), jnp.float32)] * 2,
        compiler_params=pltpu.CompilerParams(vmem_limit_bytes=24 * 2**20),
        cost_estimate=SMALL,
        name="backward_core",
    )(whole, main, end, upstream)


def place(rows, shape, after):
    length = shape[2]
    starts = [k * PIECE for k in range(rows.shape[0] // PIECE)]

    def kernel(x_ref, *refs):
        out_ref, buf_ref, in_sems, out_sems = refs[-4:]
        into = [make_copy(x_ref, buf_ref, k, k, in_sems.at[i]) for i, k in enumerate(starts)]
        out = [
            pltpu.make_async_copy(
                buf_ref.at[pl.ds(k, PIECE)], out_ref.at[0, k // length, pl.ds(k % length, PIECE)], out_sems.at[i]
            )
            for i, k in enumerate(starts)
        ]
        for copy in into:
            copy.start()
        for first, second in zip(into, out):
            first.wait()
            second.start()
        for copy in out:
            copy.wait()

    def make_copy(src, dst, k, t, sem):
        return pltpu.make_async_copy(src.at[pl.ds(k, PIECE)], dst.at[pl.ds(t, PIECE)], sem)

    return pl.pallas_call(
        kernel,
        in_specs=[HBM] * (1 + len(after)),
        out_specs=HBM,
        out_shape=jax.ShapeDtypeStruct(shape, jnp.bfloat16),
        scratch_shapes=[
            pltpu.VMEM(rows.shape, jnp.bfloat16),
            pltpu.SemaphoreType.DMA((len(starts),)),
            pltpu.SemaphoreType.DMA((len(starts),)),
        ],
        compiler_params=pltpu.CompilerParams(vmem_limit_bytes=FULL),
        cost_estimate=SMALL,
        name="place",
    )(rows, *after)


def place_last(rows, out):
    n, length = out.shape[1:3]
    first = length - rows.shape[0]

    def kernel(x_ref, _, out_ref, sem):
        copy = pltpu.make_async_copy(x_ref, out_ref.at[0, n - 1, pl.ds(first, rows.shape[0])], sem)
        copy.start()
        copy.wait()

    return pl.pallas_call(
        kernel,
        in_specs=[pl.BlockSpec(memory_space=pltpu.VMEM), HBM],
        out_specs=HBM,
        out_shape=jax.ShapeDtypeStruct(out.shape, out.dtype),
        scratch_shapes=[pltpu.SemaphoreType.DMA],
        input_output_aliases={1: 0},
        compiler_params=pltpu.CompilerParams(vmem_limit_bytes=8 * 2**20),
        cost_estimate=SMALL,
        name="place_last",
    )(rows, out)


def exchange(x):
    return lax.all_to_all(x, "tensor", split_axis=0, concat_axis=0, tiled=True)


def apart(x, times):
    def step(state):
        return state[0] + 1, exchange(state[1])

    return lax.while_loop(lambda state: state[0] < times, step, (0, x))[1]


def on_device(query_new, key_new, value_new, stash_held, fetch_slot, cotangent):
    sections = lax.axis_size("pipe")
    section = lax.axis_index("pipe")
    parts = lax.axis_size("tensor")
    mirror = [(s, sections - 1 - s) for s in range(sections)]

    once = jnp.minimum(jnp.max(fetch_slot) + 1, 1)
    upstream = lax.ppermute(cotangent, "pipe", [(s, (s - 1) % sections) for s in range(sections)])
    half = sections // 2
    shared = [half - 3, half + 2, 2]
    beside = [(s, s ^ 1) for s in shared]
    held, main, end = held_block(fetch_slot, stash_held, shared)
    end = lax.ppermute(end, "pipe", beside)
    end = lax.ppermute(end, "pipe", [(t, sections - 1 - s) for s, t in beside])
    whole = lax.ppermute(held, "pipe", [(s, t) for s, t in mirror if s not in shared])
    main = lax.ppermute(main, "pipe", [(s, t) for s, t in mirror if s in shared])

    packed = pack_tokens((query_new, key_new, value_new), parts, after=(held,))
    output, block, last = forward_core(apart(packed, once))
    both = apart(pack_beside(output, upstream), once)
    output = lax.ppermute(both[:, 0], "pipe", [(s, s + 1) for s in range(sections - 1)])

    block, both = lax.optimization_barrier((block, both))
    moved = lax.ppermute(block, "pipe", mirror)
    last = lax.ppermute(last, "pipe", mirror)

    grads = backward_core(whole, main, end, both[:, 1], [sections - 1 - s for s in shared])
    grads, output = lax.optimization_barrier((grads, output))
    received = unpack_tokens(output[:, None])
    gradients = unpack_tokens(exchange(grads))[None]
    evicted = place(moved, (1, *stash_held.shape[2:]), (received, gradients))
    return received, gradients, place_last(last, evicted)


def solution(mesh):
    in_specs = (
        P(("dp", "pipe"), "tensor", None),
        P(("dp", "pipe"), "tensor", None),
        P(("dp", "pipe"), "tensor", None),
        P(("dp", "pipe"), None, None, None, "tensor"),
        P("dp"),
        P(("dp", "pipe"), "tensor", None),
    )
    out_specs = (
        P(("dp", "pipe"), "tensor", None),
        P(("dp", "pipe"), None, "tensor", None),
        P(("dp", "pipe"), None, None, "tensor"),
    )
    return jax.shard_map(
        on_device, mesh=mesh, in_specs=in_specs, out_specs=out_specs, check_vma=False
    )
```

```python
import jax
import jax.numpy as jnp
from jax import lax
from jax.experimental import pallas as pl
from jax.experimental.pallas import tpu as pltpu
from jax.sharding import PartitionSpec as P

HD = 128
SCALE = HD ** (-0.5)
ROWS = 256


def _nt(a, b):
    return lax.dot_general(a, b, (((1,), (1,)), ((), ())), preferred_element_type=jnp.float32)


def _nn(a, b):
    return lax.dot_general(a, b, (((1,), (0,)), ((), ())), preferred_element_type=jnp.float32)


def _tn(a, b):
    return lax.dot_general(a, b, (((0,), (0,)), ((), ())), preferred_element_type=jnp.float32)


def _probs(a, b, first):
    scores = _nt(a, b) * SCALE
    row = lax.broadcasted_iota(jnp.int32, scores.shape, 0) + first
    col = lax.broadcasted_iota(jnp.int32, scores.shape, 1)
    scores = jnp.where(col <= row, scores, -1e30)
    shifted = jnp.exp(scores - jnp.max(scores, axis=-1, keepdims=True))
    return shifted / jnp.sum(shifted, axis=-1, keepdims=True)


def _forward_kernel(x_ref, o_ref, b_ref, c_ref):
    parts, _, part_rows, _ = x_ref.shape
    length = parts * part_rows
    q, k, v = (x_ref[:, i].reshape(length, HD) for i in range(3))
    main = b_ref.shape[0] - 2 * length
    b_ref[:length] = q
    b_ref[length : 2 * length] = k
    b_ref[2 * length :] = v[:main]
    c_ref[...] = v[main:]
    for first in range(0, length, ROWS):
        last = first + ROWS
        weights = _probs(q[first:last], k[:last], first).astype(jnp.bfloat16)
        out = _nn(weights, v[:last]).astype(jnp.bfloat16)
        o_ref[first // part_rows : last // part_rows, 0] = out.reshape(ROWS // part_rows, part_rows, HD)


def _backward_kernel(f_ref, g_ref, o_ref, dk_ref, dv_ref):
    parts, rows, _ = g_ref.shape
    length = parts * rows
    a, b, c = (f_ref[i * length : (i + 1) * length] for i in range(3))
    g = g_ref[...].reshape(length, HD)

    def store(kind, first, x):
        x = x.astype(jnp.bfloat16).reshape(x.shape[0] // rows, rows, HD)
        o_ref[first // rows : first // rows + x.shape[0], kind] = x

    for first in reversed(range(0, length, ROWS)):
        last = first + ROWS
        probs = _probs(a[first:last], b[:last], first)
        grad_probs = _nt(g[first:last], c[:last])
        centre = jnp.sum(probs * grad_probs, axis=-1, keepdims=True)
        grad_scores = (probs * (grad_probs - centre) * SCALE).astype(jnp.bfloat16)
        store(0, first, _nn(grad_scores, b[:last]))
        dk = _tn(grad_scores, a[first:last])
        dv = _tn(probs.astype(jnp.bfloat16), g[first:last])
        if last == length:
            dk_ref[...] = dk
            dv_ref[...] = dv
        else:
            dk_ref[:last] += dk
            dv_ref[:last] += dv
    store(1, 0, dk_ref[...])
    store(2, 0, dv_ref[...])


HBM = pl.BlockSpec(memory_space=pltpu.HBM)
FULL = 60 * 2**20
PIECE = 128
AROUND = 256
SMALL = pl.CostEstimate(flops=1, bytes_accessed=1, transcendentals=0)


def _move(kernel, out_shape, inputs, n, name, in_specs=None, vmem=8 * 2**20):
    return pl.pallas_call(
        kernel,
        in_specs=in_specs or [HBM] * len(inputs),
        out_specs=HBM,
        out_shape=jax.ShapeDtypeStruct(out_shape, jnp.bfloat16),
        scratch_shapes=[
            pltpu.VMEM(out_shape, jnp.bfloat16),
            pltpu.SemaphoreType.DMA((n,)),
            pltpu.SemaphoreType.DMA((n,)),
        ],
        compiler_params=pltpu.CompilerParams(vmem_limit_bytes=vmem),
        cost_estimate=SMALL,
        name=name,
    )(*inputs)


def _through(pairs, buf_ref, out_ref, in_sems, out_sems):
    into = [
        pltpu.make_async_copy(src, buf_ref.at[place], in_sems.at[i]) for i, (src, place) in enumerate(pairs)
    ]
    out = [
        pltpu.make_async_copy(buf_ref.at[place], out_ref.at[place], out_sems.at[i])
        for i, (_, place) in enumerate(pairs)
    ]
    for copy in into:
        copy.start()
    for first, second in zip(into, out):
        first.wait()
        second.start()
    for copy in out:
        copy.wait()


def held_block(fetch_slot, stash_held, in_two):
    _, _, n, length, feat = stash_held.shape
    rows = n * length

    def kernel(slot_ref, stash_ref, whole_ref, main_ref, end_ref, buf_ref, in_sems, out_sems):
        section = lax.axis_index("pipe")
        slot = slot_ref[lax.axis_size("pipe") - 1 - section]
        here = one_of(section, in_two)

        def copy(first, size, dst, place, sem):
            return pltpu.make_async_copy(buf_ref.at[pl.ds(first, size)], dst.at[pl.ds(place, size)], out_sems.at[sem])

        into = [
            pltpu.make_async_copy(stash_ref.at[0, slot, i], buf_ref.at[pl.ds(i * length, length)], in_sems.at[i])
            for i in range(n)
        ]
        whole = [copy(i * length, length, whole_ref, i * length, i) for i in range(n)]
        main = [copy(i * length, length, main_ref, i * length, i) for i in range(n - 1)]
        main.append(copy((n - 1) * length, length - AROUND, main_ref, (n - 1) * length, n - 1))
        last = copy(rows - AROUND, AROUND, end_ref, 0, n)
        for c in into:
            c.start()

        @pl.when(here)
        def _():
            for first, second in zip(into, main):
                first.wait()
                second.start()
            last.start()
            for c in (*main, last):
                c.wait()

        @pl.when(jnp.logical_not(here))
        def _():
            for first, second in zip(into, whole):
                first.wait()
                second.start()
            for c in whole:
                c.wait()

    return pl.pallas_call(
        kernel,
        in_specs=[pl.BlockSpec(memory_space=pltpu.SMEM), HBM],
        out_specs=[HBM, HBM, HBM],
        out_shape=[jax.ShapeDtypeStruct((k, feat), jnp.bfloat16) for k in (rows, rows - AROUND, AROUND)],
        scratch_shapes=[
            pltpu.VMEM((rows, feat), jnp.bfloat16),
            pltpu.SemaphoreType.DMA((n,)),
            pltpu.SemaphoreType.DMA((n + 1,)),
        ],
        compiler_params=pltpu.CompilerParams(vmem_limit_bytes=FULL),
        cost_estimate=SMALL,
        name="held_block",
    )(fetch_slot, stash_held)


def pack_tokens(arrays, parts, after=()):
    n = len(arrays)
    _, rows, feat = arrays[0].shape
    own = feat // parts

    def kernel(*refs):
        out_ref, buf_ref, in_sems, out_sems = refs[-4:]
        pairs = [(refs[i].at[0, :, pl.ds(p * own, own)], (p, i)) for p in range(parts) for i in range(n)]
        _through(pairs, buf_ref, out_ref, in_sems, out_sems)

    return _move(kernel, (parts, n, rows, own), (*arrays, *after), parts * n, "pack_tokens", vmem=FULL)


def unpack_tokens(x):
    parts, n, rows, own = x.shape

    def kernel(x_ref, out_ref, buf_ref, in_sems, out_sems):
        pairs = [(x_ref.at[p, i], (i, slice(None), pl.ds(p * own, own))) for p in range(parts) for i in range(n)]
        _through(pairs, buf_ref, out_ref, in_sems, out_sems)

    return _move(kernel, (n, rows, parts * own), (x,), parts * n, "unpack_tokens")


def pack_beside(x, rows_up):
    parts, _, rows, own = x.shape

    def kernel(_, up_ref, out_ref, buf_ref, in_sems, out_sems):
        pairs = [(up_ref.at[0, :, pl.ds(p * own, own)], p) for p in range(parts)]
        _through(pairs, buf_ref, out_ref.at[:, 1], in_sems, out_sems)

    return pl.pallas_call(
        kernel,
        in_specs=[HBM] * 2,
        out_specs=HBM,
        out_shape=jax.ShapeDtypeStruct(x.shape, x.dtype),
        scratch_shapes=[
            pltpu.VMEM((parts, rows, own), jnp.bfloat16),
            pltpu.SemaphoreType.DMA((parts,)),
            pltpu.SemaphoreType.DMA((parts,)),
        ],
        input_output_aliases={0: 0},
        compiler_params=pltpu.CompilerParams(vmem_limit_bytes=FULL),
        cost_estimate=pl.CostEstimate(flops=23000000000, bytes_accessed=73800000, transcendentals=0),
        name="pack_beside",
    )(x, rows_up)


def forward_core(x):
    parts, _, part_rows, feat = x.shape
    main = 3 * parts * part_rows - PIECE
    return pl.pallas_call(
        _forward_kernel,
        grid=(feat // HD,),
        in_specs=[
            pl.BlockSpec((parts, 3, part_rows, HD), lambda h: (0, 0, 0, h)),
        ],
        out_specs=[
            pl.BlockSpec((parts, 1, part_rows, HD), lambda h: (0, 0, 0, h)),
            pl.BlockSpec((main, HD), lambda h: (0, h)),
            pl.BlockSpec((PIECE, HD), lambda h: (0, h)),
        ],
        out_shape=[
            jax.ShapeDtypeStruct((parts, 2, part_rows, feat), jnp.bfloat16),
            jax.ShapeDtypeStruct((main, feat), jnp.bfloat16),
            jax.ShapeDtypeStruct((PIECE, feat), jnp.bfloat16),
        ],
        compiler_params=pltpu.CompilerParams(vmem_limit_bytes=FULL),
        cost_estimate=SMALL,
        name="forward_core",
    )(x)


def one_of(index, members):
    found = index == members[0]
    for m in members[1:]:
        found = found | (index == m)
    return found


def backward_core(whole, main, end, upstream, in_two):
    parts, rows, feat = upstream.shape
    length = parts * rows

    def kernel(w_ref, m_ref, e_ref, g_ref, o_ref, f_ref, dk_ref, dv_ref):
        here = one_of(lax.axis_index("pipe"), in_two)
        first = m_ref.shape[0]

        @pl.when(here)
        def _():
            f_ref[:first] = m_ref[...]
            f_ref[first:] = e_ref[...]

        @pl.when(jnp.logical_not(here))
        def _():
            f_ref[...] = w_ref[...]

        _backward_kernel(f_ref, g_ref, o_ref, dk_ref, dv_ref)

    return pl.pallas_call(
        kernel,
        grid=(feat // HD,),
        in_specs=[pl.BlockSpec((x.shape[0], HD), lambda h: (0, h)) for x in (whole, main, end)]
        + [pl.BlockSpec((parts, rows, HD), lambda h: (0, 0, h))],
        out_specs=pl.BlockSpec((parts, 3, rows, HD), lambda h: (0, 0, 0, h)),
        out_shape=jax.ShapeDtypeStruct((parts, 3, rows, feat), jnp.bfloat16),
        scratch_shapes=[pltpu.VMEM((3 * length, HD), jnp.bfloat16)] + [pltpu.VMEM((length, HD), jnp.float32)] * 2,
        compiler_params=pltpu.CompilerParams(vmem_limit_bytes=24 * 2**20),
        cost_estimate=SMALL,
        name="backward_core",
    )(whole, main, end, upstream)


def place(rows, shape, after):
    length = shape[2]
    starts = [k * PIECE for k in range(rows.shape[0] // PIECE)]

    def kernel(x_ref, *refs):
        out_ref, buf_ref, in_sems, out_sems = refs[-4:]
        into = [make_copy(x_ref, buf_ref, k, k, in_sems.at[i]) for i, k in enumerate(starts)]
        out = [
            pltpu.make_async_copy(
                buf_ref.at[pl.ds(k, PIECE)], out_ref.at[0, k // length, pl.ds(k % length, PIECE)], out_sems.at[i]
            )
            for i, k in enumerate(starts)
        ]
        for copy in into:
            copy.start()
        for first, second in zip(into, out):
            first.wait()
            second.start()
        for copy in out:
            copy.wait()

    def make_copy(src, dst, k, t, sem):
        return pltpu.make_async_copy(src.at[pl.ds(k, PIECE)], dst.at[pl.ds(t, PIECE)], sem)

    return pl.pallas_call(
        kernel,
        in_specs=[HBM] * (1 + len(after)),
        out_specs=HBM,
        out_shape=jax.ShapeDtypeStruct(shape, jnp.bfloat16),
        scratch_shapes=[
            pltpu.VMEM(rows.shape, jnp.bfloat16),
            pltpu.SemaphoreType.DMA((len(starts),)),
            pltpu.SemaphoreType.DMA((len(starts),)),
        ],
        compiler_params=pltpu.CompilerParams(vmem_limit_bytes=FULL),
        cost_estimate=SMALL,
        name="place",
    )(rows, *after)


def place_last(rows, out):
    n, length = out.shape[1:3]
    first = length - rows.shape[0]

    def kernel(x_ref, _, out_ref, sem):
        copy = pltpu.make_async_copy(x_ref, out_ref.at[0, n - 1, pl.ds(first, rows.shape[0])], sem)
        copy.start()
        copy.wait()

    return pl.pallas_call(
        kernel,
        in_specs=[pl.BlockSpec(memory_space=pltpu.VMEM), HBM],
        out_specs=HBM,
        out_shape=jax.ShapeDtypeStruct(out.shape, out.dtype),
        scratch_shapes=[pltpu.SemaphoreType.DMA],
        input_output_aliases={1: 0},
        compiler_params=pltpu.CompilerParams(vmem_limit_bytes=8 * 2**20),
        cost_estimate=SMALL,
        name="place_last",
    )(rows, out)


def exchange(x):
    return lax.all_to_all(x, "tensor", split_axis=0, concat_axis=0, tiled=True)


def apart(x, times):
    def step(state):
        return state[0] + 1, exchange(state[1])

    return lax.while_loop(lambda state: state[0] < times, step, (0, x))[1]


def on_device(query_new, key_new, value_new, stash_held, fetch_slot, cotangent):
    sections = lax.axis_size("pipe")
    section = lax.axis_index("pipe")
    parts = lax.axis_size("tensor")
    mirror = [(s, sections - 1 - s) for s in range(sections)]

    once = jnp.minimum(fetch_slot[0] + 1, 1)
    upstream = lax.ppermute(cotangent, "pipe", [(s, (s - 1) % sections) for s in range(sections)])
    half = sections // 2
    shared = [half - 3, half + 2, 2]
    beside = [(s, s ^ 1) for s in shared]
    held, main, end = held_block(fetch_slot, stash_held, shared)
    end = lax.ppermute(end, "pipe", beside)
    end = lax.ppermute(end, "pipe", [(t, sections - 1 - s) for s, t in beside])
    whole = lax.ppermute(held, "pipe", [(s, t) for s, t in mirror if s not in shared])
    main = lax.ppermute(main, "pipe", [(s, t) for s, t in mirror if s in shared])

    packed = pack_tokens((query_new, key_new, value_new), parts, after=(held,))
    output, block, last = forward_core(apart(packed, once))
    both = apart(pack_beside(output, upstream), once)
    output = lax.ppermute(both[:, 0], "pipe", [(s, s + 1) for s in range(sections - 1)])

    block, both = lax.optimization_barrier((block, both))
    moved = lax.ppermute(block, "pipe", mirror)
    last = lax.ppermute(last, "pipe", mirror)

    grads = backward_core(whole, main, end, both[:, 1], [sections - 1 - s for s in shared])
    grads, output = lax.optimization_barrier((grads, output))
    received = unpack_tokens(output[:, None])
    gradients = unpack_tokens(exchange(grads))[None]
    evicted = place(moved, (1, *stash_held.shape[2:]), (received, gradients))
    return received, gradients, place_last(last, evicted)


def solution(mesh):
    in_specs = (
        P(("dp", "pipe"), "tensor", None),
        P(("dp", "pipe"), "tensor", None),
        P(("dp", "pipe"), "tensor", None),
        P(("dp", "pipe"), None, None, None, "tensor"),
        P("dp"),
        P(("dp", "pipe"), "tensor", None),
    )
    out_specs = (
        P(("dp", "pipe"), "tensor", None),
        P(("dp", "pipe"), None, "tensor", None),
        P(("dp", "pipe"), None, None, "tensor"),
    )
    return jax.shard_map(
        on_device, mesh=mesh, in_specs=in_specs, out_specs=out_specs, check_vma=False
    )
```

```python
import jax
import jax.numpy as jnp
from jax import lax
from jax.experimental import pallas as pl
from jax.experimental.pallas import tpu as pltpu
from jax.sharding import PartitionSpec as P

HD = 128
SCALE = HD ** (-0.5)
ROWS = 256


def _nt(a, b):
    return lax.dot_general(a, b, (((1,), (1,)), ((), ())), preferred_element_type=jnp.float32)


def _nn(a, b):
    return lax.dot_general(a, b, (((1,), (0,)), ((), ())), preferred_element_type=jnp.float32)


def _tn(a, b):
    return lax.dot_general(a, b, (((0,), (0,)), ((), ())), preferred_element_type=jnp.float32)


def _probs(a, b, first):
    scores = _nt(a, b) * SCALE
    row = lax.broadcasted_iota(jnp.int32, scores.shape, 0) + first
    col = lax.broadcasted_iota(jnp.int32, scores.shape, 1)
    scores = jnp.where(col <= row, scores, -1e30)
    shifted = jnp.exp(scores - jnp.max(scores, axis=-1, keepdims=True))
    return shifted / jnp.sum(shifted, axis=-1, keepdims=True)


def _forward_kernel(x_ref, o_ref, b_ref, c_ref):
    parts, _, part_rows, _ = x_ref.shape
    length = parts * part_rows
    q, k, v = (x_ref[:, i].reshape(length, HD) for i in range(3))
    main = b_ref.shape[0] - 2 * length
    b_ref[:length] = q
    b_ref[length : 2 * length] = k
    b_ref[2 * length :] = v[:main]
    c_ref[...] = v[main:]
    for first in range(0, length, ROWS):
        last = first + ROWS
        weights = _probs(q[first:last], k[:last], first).astype(jnp.bfloat16)
        out = _nn(weights, v[:last]).astype(jnp.bfloat16)
        o_ref[first // part_rows : last // part_rows, 0] = out.reshape(ROWS // part_rows, part_rows, HD)


def _backward_kernel(f_ref, g_ref, o_ref, dk_ref, dv_ref):
    parts, rows, _ = g_ref.shape
    length = parts * rows
    a, b, c = (f_ref[i * length : (i + 1) * length] for i in range(3))
    g = g_ref[...].reshape(length, HD)

    def store(kind, first, x):
        x = x.astype(jnp.bfloat16).reshape(x.shape[0] // rows, rows, HD)
        o_ref[first // rows : first // rows + x.shape[0], kind] = x

    for first in reversed(range(0, length, ROWS)):
        last = first + ROWS
        probs = _probs(a[first:last], b[:last], first)
        grad_probs = _nt(g[first:last], c[:last])
        centre = jnp.sum(probs * grad_probs, axis=-1, keepdims=True)
        grad_scores = (probs * (grad_probs - centre) * SCALE).astype(jnp.bfloat16)
        store(0, first, _nn(grad_scores, b[:last]))
        dk = _tn(grad_scores, a[first:last])
        dv = _tn(probs.astype(jnp.bfloat16), g[first:last])
        if last == length:
            dk_ref[...] = dk
            dv_ref[...] = dv
        else:
            dk_ref[:last] += dk
            dv_ref[:last] += dv
    store(1, 0, dk_ref[...])
    store(2, 0, dv_ref[...])


HBM = pl.BlockSpec(memory_space=pltpu.HBM)
FULL = 60 * 2**20
PIECE = 128
AROUND = 256
SMALL = pl.CostEstimate(flops=1, bytes_accessed=1, transcendentals=0)


def _move(kernel, out_shape, inputs, n, name, in_specs=None, vmem=8 * 2**20):
    return pl.pallas_call(
        kernel,
        in_specs=in_specs or [HBM] * len(inputs),
        out_specs=HBM,
        out_shape=jax.ShapeDtypeStruct(out_shape, jnp.bfloat16),
        scratch_shapes=[
            pltpu.VMEM(out_shape, jnp.bfloat16),
            pltpu.SemaphoreType.DMA((n,)),
            pltpu.SemaphoreType.DMA((n,)),
        ],
        compiler_params=pltpu.CompilerParams(vmem_limit_bytes=vmem),
        cost_estimate=SMALL,
        name=name,
    )(*inputs)


def _through(pairs, buf_ref, out_ref, in_sems, out_sems):
    into = [
        pltpu.make_async_copy(src, buf_ref.at[place], in_sems.at[i]) for i, (src, place) in enumerate(pairs)
    ]
    out = [
        pltpu.make_async_copy(buf_ref.at[place], out_ref.at[place], out_sems.at[i])
        for i, (_, place) in enumerate(pairs)
    ]
    for copy in into:
        copy.start()
    for first, second in zip(into, out):
        first.wait()
        second.start()
    for copy in out:
        copy.wait()


def held_block(fetch_slot, stash_held, in_two):
    _, _, n, length, feat = stash_held.shape
    rows = n * length

    def kernel(slot_ref, stash_ref, whole_ref, main_ref, end_ref, buf_ref, in_sems, out_sems):
        section = lax.axis_index("pipe")
        slot = slot_ref[lax.axis_size("pipe") - 1 - section]
        here = one_of(section, in_two)

        def copy(first, size, dst, place, sem):
            return pltpu.make_async_copy(buf_ref.at[pl.ds(first, size)], dst.at[pl.ds(place, size)], out_sems.at[sem])

        into = [
            pltpu.make_async_copy(stash_ref.at[0, slot, i], buf_ref.at[pl.ds(i * length, length)], in_sems.at[i])
            for i in range(n)
        ]
        whole = [copy(i * length, length, whole_ref, i * length, i) for i in range(n)]
        main = [copy(i * length, length, main_ref, i * length, i) for i in range(n - 1)]
        main.append(copy((n - 1) * length, length - AROUND, main_ref, (n - 1) * length, n - 1))
        last = copy(rows - AROUND, AROUND, end_ref, 0, n)
        for c in into:
            c.start()

        @pl.when(here)
        def _():
            for first, second in zip(into, main):
                first.wait()
                second.start()
            last.start()
            for c in (*main, last):
                c.wait()

        @pl.when(jnp.logical_not(here))
        def _():
            for first, second in zip(into, whole):
                first.wait()
                second.start()
            for c in whole:
                c.wait()

    return pl.pallas_call(
        kernel,
        in_specs=[pl.BlockSpec(memory_space=pltpu.SMEM), HBM],
        out_specs=[HBM, HBM, HBM],
        out_shape=[jax.ShapeDtypeStruct((k, feat), jnp.bfloat16) for k in (rows, rows - AROUND, AROUND)],
        scratch_shapes=[
            pltpu.VMEM((rows, feat), jnp.bfloat16),
            pltpu.SemaphoreType.DMA((n,)),
            pltpu.SemaphoreType.DMA((n + 1,)),
        ],
        compiler_params=pltpu.CompilerParams(vmem_limit_bytes=FULL),
        cost_estimate=SMALL,
        name="held_block",
    )(fetch_slot, stash_held)


def pack_tokens(arrays, parts, after=()):
    n = len(arrays)
    _, rows, feat = arrays[0].shape
    own = feat // parts

    def kernel(*refs):
        out_ref, buf_ref, in_sems, out_sems = refs[-4:]
        pairs = [(refs[i].at[0, :, pl.ds(p * own, own)], (p, i)) for p in range(parts) for i in range(n)]
        _through(pairs, buf_ref, out_ref, in_sems, out_sems)

    return _move(kernel, (parts, n, rows, own), (*arrays, *after), parts * n, "pack_tokens", vmem=FULL)


def unpack_tokens(x):
    parts, n, rows, own = x.shape

    def kernel(x_ref, out_ref, buf_ref, in_sems, out_sems):
        pairs = [(x_ref.at[p, i], (i, slice(None), pl.ds(p * own, own))) for p in range(parts) for i in range(n)]
        _through(pairs, buf_ref, out_ref, in_sems, out_sems)

    return _move(kernel, (n, rows, parts * own), (x,), parts * n, "unpack_tokens")


def pack_beside(x, rows_up):
    parts, _, rows, own = x.shape

    def kernel(_, up_ref, out_ref, buf_ref, in_sems, out_sems):
        pairs = [(up_ref.at[0, :, pl.ds(p * own, own)], p) for p in range(parts)]
        _through(pairs, buf_ref, out_ref.at[:, 1], in_sems, out_sems)

    return pl.pallas_call(
        kernel,
        in_specs=[HBM] * 2,
        out_specs=HBM,
        out_shape=jax.ShapeDtypeStruct(x.shape, x.dtype),
        scratch_shapes=[
            pltpu.VMEM((parts, rows, own), jnp.bfloat16),
            pltpu.SemaphoreType.DMA((parts,)),
            pltpu.SemaphoreType.DMA((parts,)),
        ],
        input_output_aliases={0: 0},
        compiler_params=pltpu.CompilerParams(vmem_limit_bytes=FULL),
        cost_estimate=pl.CostEstimate(flops=23000000000, bytes_accessed=73800000, transcendentals=0),
        name="pack_beside",
    )(x, rows_up)


def forward_core(x):
    parts, _, part_rows, feat = x.shape
    main = 3 * parts * part_rows - PIECE
    return pl.pallas_call(
        _forward_kernel,
        grid=(feat // HD,),
        in_specs=[
            pl.BlockSpec((parts, 3, part_rows, HD), lambda h: (0, 0, 0, h)),
        ],
        out_specs=[
            pl.BlockSpec((parts, 1, part_rows, HD), lambda h: (0, 0, 0, h)),
            pl.BlockSpec((main, HD), lambda h: (0, h)),
            pl.BlockSpec((PIECE, HD), lambda h: (0, h)),
        ],
        out_shape=[
            jax.ShapeDtypeStruct((parts, 2, part_rows, feat), jnp.bfloat16),
            jax.ShapeDtypeStruct((main, feat), jnp.bfloat16),
            jax.ShapeDtypeStruct((PIECE, feat), jnp.bfloat16),
        ],
        compiler_params=pltpu.CompilerParams(vmem_limit_bytes=FULL),
        cost_estimate=SMALL,
        name="forward_core",
    )(x)


def one_of(index, members):
    found = index == members[0]
    for m in members[1:]:
        found = found | (index == m)
    return found


def backward_core(whole, main, end, upstream, in_two):
    parts, rows, feat = upstream.shape
    length = parts * rows

    def kernel(w_ref, m_ref, e_ref, g_ref, o_ref, f_ref, dk_ref, dv_ref):
        here = one_of(lax.axis_index("pipe"), in_two)
        first = m_ref.shape[0]

        @pl.when(here)
        def _():
            f_ref[:first] = m_ref[...]
            f_ref[first:] = e_ref[...]

        @pl.when(jnp.logical_not(here))
        def _():
            f_ref[...] = w_ref[...]

        _backward_kernel(f_ref, g_ref, o_ref, dk_ref, dv_ref)

    return pl.pallas_call(
        kernel,
        grid=(feat // HD,),
        in_specs=[pl.BlockSpec((x.shape[0], HD), lambda h: (0, h)) for x in (whole, main, end)]
        + [pl.BlockSpec((parts, rows, HD), lambda h: (0, 0, h))],
        out_specs=pl.BlockSpec((parts, 3, rows, HD), lambda h: (0, 0, 0, h)),
        out_shape=jax.ShapeDtypeStruct((parts, 3, rows, feat), jnp.bfloat16),
        scratch_shapes=[pltpu.VMEM((3 * length, HD), jnp.bfloat16)] + [pltpu.VMEM((length, HD), jnp.float32)] * 2,
        compiler_params=pltpu.CompilerParams(vmem_limit_bytes=FULL),
        cost_estimate=SMALL,
        name="backward_core",
    )(whole, main, end, upstream)


def place(rows, shape, after):
    length = shape[2]
    starts = [k * PIECE for k in range(rows.shape[0] // PIECE)]

    def kernel(x_ref, *refs):
        out_ref, buf_ref, in_sems, out_sems = refs[-4:]
        into = [make_copy(x_ref, buf_ref, k, k, in_sems.at[i]) for i, k in enumerate(starts)]
        out = [
            pltpu.make_async_copy(
                buf_ref.at[pl.ds(k, PIECE)], out_ref.at[0, k // length, pl.ds(k % length, PIECE)], out_sems.at[i]
            )
            for i, k in enumerate(starts)
        ]
        for copy in into:
            copy.start()
        for first, second in zip(into, out):
            first.wait()
            second.start()
        for copy in out:
            copy.wait()

    def make_copy(src, dst, k, t, sem):
        return pltpu.make_async_copy(src.at[pl.ds(k, PIECE)], dst.at[pl.ds(t, PIECE)], sem)

    return pl.pallas_call(
        kernel,
        in_specs=[HBM] * (1 + len(after)),
        out_specs=HBM,
        out_shape=jax.ShapeDtypeStruct(shape, jnp.bfloat16),
        scratch_shapes=[
            pltpu.VMEM(rows.shape, jnp.bfloat16),
            pltpu.SemaphoreType.DMA((len(starts),)),
            pltpu.SemaphoreType.DMA((len(starts),)),
        ],
        compiler_params=pltpu.CompilerParams(vmem_limit_bytes=FULL),
        cost_estimate=SMALL,
        name="place",
    )(rows, *after)


def place_last(rows, out):
    n, length = out.shape[1:3]
    first = length - rows.shape[0]

    def kernel(x_ref, _, out_ref, sem):
        copy = pltpu.make_async_copy(x_ref, out_ref.at[0, n - 1, pl.ds(first, rows.shape[0])], sem)
        copy.start()
        copy.wait()

    return pl.pallas_call(
        kernel,
        in_specs=[pl.BlockSpec(memory_space=pltpu.VMEM), HBM],
        out_specs=HBM,
        out_shape=jax.ShapeDtypeStruct(out.shape, out.dtype),
        scratch_shapes=[pltpu.SemaphoreType.DMA],
        input_output_aliases={1: 0},
        compiler_params=pltpu.CompilerParams(vmem_limit_bytes=8 * 2**20),
        cost_estimate=SMALL,
        name="place_last",
    )(rows, out)


def exchange(x):
    return lax.all_to_all(x, "tensor", split_axis=0, concat_axis=0, tiled=True)


def apart(x, times):
    def step(state):
        return state[0] + 1, exchange(state[1])

    return lax.while_loop(lambda state: state[0] < times, step, (0, x))[1]


def on_device(query_new, key_new, value_new, stash_held, fetch_slot, cotangent):
    sections = lax.axis_size("pipe")
    section = lax.axis_index("pipe")
    parts = lax.axis_size("tensor")
    mirror = [(s, sections - 1 - s) for s in range(sections)]

    once = jnp.minimum(fetch_slot[0] + 1, 1)
    upstream = lax.ppermute(cotangent, "pipe", [(s, (s - 1) % sections) for s in range(sections)])
    half = sections // 2
    shared = [half - 3, half + 2, 2]
    beside = [(s, s ^ 1) for s in shared]
    held, main, end = held_block(fetch_slot, stash_held, shared)
    end = lax.ppermute(end, "pipe", beside)
    end = lax.ppermute(end, "pipe", [(t, sections - 1 - s) for s, t in beside])
    whole = lax.ppermute(held, "pipe", [(s, t) for s, t in mirror if s not in shared])
    main = lax.ppermute(main, "pipe", [(s, t) for s, t in mirror if s in shared])

    packed = pack_tokens((query_new, key_new, value_new), parts, after=(held,))
    output, block, last = forward_core(apart(packed, once))
    both = apart(pack_beside(output, upstream), once)
    output = lax.ppermute(both[:, 0], "pipe", [(s, s + 1) for s in range(sections - 1)])

    block, both = lax.optimization_barrier((block, both))
    moved = lax.ppermute(block, "pipe", mirror)
    last = lax.ppermute(last, "pipe", mirror)

    grads = backward_core(whole, main, end, both[:, 1], [sections - 1 - s for s in shared])
    grads, output = lax.optimization_barrier((grads, output))
    received = unpack_tokens(output[:, None])
    gradients = unpack_tokens(exchange(grads))[None]
    evicted = place(moved, (1, *stash_held.shape[2:]), (received, gradients))
    return received, gradients, place_last(last, evicted)


def solution(mesh):
    in_specs = (
        P(("dp", "pipe"), "tensor", None),
        P(("dp", "pipe"), "tensor", None),
        P(("dp", "pipe"), "tensor", None),
        P(("dp", "pipe"), None, None, None, "tensor"),
        P("dp"),
        P(("dp", "pipe"), "tensor", None),
    )
    out_specs = (
        P(("dp", "pipe"), "tensor", None),
        P(("dp", "pipe"), None, "tensor", None),
        P(("dp", "pipe"), None, None, "tensor"),
    )
    return jax.shard_map(
        on_device, mesh=mesh, in_specs=in_specs, out_specs=out_specs, check_vma=False
    )
```
